256 devices in a mesh: dp: 2 (over core), ctx: 16 (over y, x), tp: 8 (over z).
Axes of the slice: x: 4, y: 4, z: 8, core: 2. Of those that a mesh axis runs over, the one named last changes fastest.
Arguments:
- queries: bfloat16 [2, 3072, 4096], P('dp', 'ctx', 'tp'), may hold values from -20 to 20
- keys: bfloat16 [2, 3072, 4096], P('dp', 'ctx', 'tp'), may hold values from -20 to 20
- values: bfloat16 [2, 3072, 4096], P('dp', 'ctx', 'tp'), may hold values from -6 to 6
- cotangent: bfloat16 [2, 3072, 4096], P('dp', 'ctx', 'tp'), may hold values from -6 to 6
- w_out: bfloat16 [4096, 4096], P('tp'), may hold values from -0.125 to 0.125
- clip_lengths: int32 [2, 3], P('dp'), may hold values from 1 to 2688, 3072 in all within a row
Outputs:
- layer_out: bfloat16 [2, 3072, 4096], P('dp', 'ctx', 'tp')
- grad_q: bfloat16 [2, 3072, 4096], P('dp', 'ctx', 'tp')
- grad_k: bfloat16 [2, 3072, 4096], P('dp', 'ctx', 'tp')
- grad_v: bfloat16 [2, 3072, 4096], P('dp', 'ctx', 'tp')
- grad_w_out: float32 [4096, 4096], P('tp', 'ctx')
The draws below stay inside these ranges and needn't reach their ends.
Inputs may be any that keep to these rules, and one draw needn't show every extreme that they name: `clip_lengths`: each group's 3 lengths sum to 3072; the longest is exactly 2688.
All inputs are finite; a program needn't handle non-finite values.
Results may differ from the reference program's by a relative error of at most 0.034.
Values may be sent and summed in bfloat16 or wider, within the bound.
No kernel may reach another device: no remote copies, remote signals or barrier semaphores. Data moves between devices by JAX's collectives and lax.ppermute only.
A program may use at most 128 MiB of HBM per device.

```python
import math
import jax
import jax.numpy as jnp
import numpy as np
from jax import lax

D = 4096
HEADS = 32
HEAD = 128
FRAME = 512
CLIPS = 3
TOKENS = 3072
CLIP_MOST = 2688
N_DP = 2


def shared_keys(key):
    return jax.random.truncated_normal(jax.random.fold_in(key, 11), -4.0, 4.0, (N_DP, TOKENS, HEADS * HEAD), jnp.float32)


def draw_keys(key, part):
    shared = shared_keys(key)
    return shared.astype(jnp.bfloat16)


def draw_queries(key, part):
    own_key = jax.random.fold_in(key, 2)
    fresh = jax.random.truncated_normal(own_key, -4.0, 4.0, (N_DP, TOKENS, HEADS * HEAD), jnp.float32)
    return fresh.astype(jnp.bfloat16)


def spiked(values, stream_key, source, target, blocks, factor):
    def block_of(dim):
        return (jnp.arange(values.shape[dim]) // (values.shape[dim] // blocks)).reshape((-1,) + (1,) * (values.ndim - 1 - dim))

    first = jax.random.permutation(stream_key, blocks)[block_of(target)]
    other_side = (block_of(target) + blocks // 2) % blocks
    return jnp.where((block_of(source) == first) | (block_of(source) == other_side), factor * values, values)


def levels(key, dims, pieces, low, largest):
    def one(dim, parts):
        heights = jax.random.uniform(jax.random.fold_in(jax.random.fold_in(key, 6), dim), (parts,), jnp.float32, low / len(pieces), largest / len(pieces))
        return jnp.repeat(jnp.exp(heights), dims[dim] // parts).reshape((-1,) + (1,) * (len(dims) - dim - 1))

    loudness = one(*pieces[0])
    for cut in pieces[1:]:
        loudness = loudness * one(*cut)
    return loudness


def profile(amount, total, bound, skew):
    portions = [(1 << 20) // math.isqrt(standing ** skew) + 1 for standing in range(2, amount + 1)]
    spare, holding = total - bound - (amount - 1), [1] * (amount - 1)
    while spare > 0:
        movable = [i for i in range(amount - 1) if holding[i] < bound]
        whole, remaining = sum([portions[i] for i in movable]), spare
        for i in movable:
            more = min(bound - holding[i], max(1, remaining * portions[i] // whole), spare)
            holding[i] = holding[i] + more
            spare = spare - more
    return np.array([bound] + holding)


def uneven_parts(rng, amount, total, limit, slope):
    if amount == 2:
        one = jax.random.randint(rng, (), max(1, total - limit), min(limit, total - 1) + 1)
        return jnp.stack([one, total - one])
    sizes = jnp.asarray(profile(amount, total, limit, slope), jnp.int32)
    twos = (amount - 1) // 2
    donor, taker = sizes[1:1 + 2 * twos:2], sizes[2:2 + 2 * twos:2]
    slack = jnp.minimum(donor - 1, limit - taker)
    moved = jax.random.randint(jax.random.fold_in(rng, 1), (twos,), 0, 1 << 20) % (slack + 1)
    sizes = sizes.at[1:1 + 2 * twos:2].set(donor - moved).at[2:2 + 2 * twos:2].set(taker + moved)
    return sizes[jax.random.permutation(jax.random.fold_in(rng, 2), amount)]


def centred(stream_key, dims, spread, most, cuts=(), held_as=jnp.bfloat16):
    values = spread * jax.random.normal(stream_key, dims, jnp.float32)
    if cuts:
        values = values * levels(stream_key, dims, cuts, -0.22, 0.18)
    return jnp.clip(values, -most, most).astype(held_as)


def bell_draw_with(stream_key, extent, width, limit, cuts, heavy, held_as=jnp.bfloat16):
    drawn = width * jax.random.normal(stream_key, extent, jnp.float32)
    if cuts:
        drawn = drawn * levels(stream_key, extent, cuts, -0.22, 0.18)
    return jnp.clip(spiked(drawn, jax.random.fold_in(stream_key, 3), *heavy), -limit, limit).astype(held_as)


def setup_inputs(seed: int = 0) -> dict:
    seeds = jax.random.split(jax.random.key(seed), 7)
    queries = draw_queries(jax.random.fold_in(seeds[6], 71), 0)
    keys = draw_keys(jax.random.fold_in(seeds[6], 71), 0)
    values = centred(seeds[2], (N_DP, TOKENS, HEADS * HEAD), 1.0, 6.0, ((0, 2), (1, 16), (2, 8)))
    cotangent = bell_draw_with(seeds[3], (N_DP, TOKENS, D), 1.0, 6.0, ((0, 2), (1, 16), (2, 8)), (1, 2, 16, 2.0))
    w_out = bell_draw_with(seeds[4], (HEADS * HEAD, D), (HEADS * HEAD) ** -0.5, 0.125, ((0, 8),), (0, 1, 8, 2.0))
    clip_lengths = jax.vmap(lambda own: uneven_parts(own, CLIPS, TOKENS, CLIP_MOST, 2))(jax.random.split(seeds[5], N_DP)).reshape((N_DP, CLIPS)).astype(jnp.int32)
    return {"queries": queries, "keys": keys, "values": values, "cotangent": cotangent, "w_out": w_out, "clip_lengths": clip_lengths}


def token_frames(clip_sizes, count):
    position = jnp.arange(count, dtype=jnp.int32)
    clip_ends = jnp.cumsum(clip_sizes).astype(jnp.int32)
    earlier = (clip_ends[None, :] <= position[:, None]).astype(jnp.int32)
    clip_id = lax.optimization_barrier(jnp.sum(earlier, axis=1)).astype(jnp.int32)
    clip_start = lax.optimization_barrier(jnp.sum(earlier * clip_sizes[None, :], axis=1)).astype(jnp.int32)
    return (clip_id, (position - clip_start) // FRAME)

def reference(queries, keys, values, cotangent, w_out, clip_lengths):
    inv_root = 1.0 / math.sqrt(HEAD)
    outputs = []
    weight_grad = jnp.zeros((HEADS * HEAD, D), jnp.float32)

    def by_head(matrix):
        return matrix.reshape(TOKENS, HEADS, HEAD).transpose(1, 0, 2)

    def merge_heads(stack):
        return stack.transpose(1, 0, 2).reshape(TOKENS, HEADS * HEAD)
    for group_index in range(N_DP):
        clip_id, frame_id = token_frames(clip_lengths[group_index], TOKENS)
        allowed = (clip_id[:, None] == clip_id[None, :]) & (frame_id[None, :] <= frame_id[:, None])
        grad_attn = jnp.dot(cotangent[group_index], w_out.T, preferred_element_type=jnp.float32).astype(jnp.bfloat16)

        def head_pass(items):
            q_head, k_head, v_head, g_head = items
            logits = jnp.dot(q_head, k_head.T, preferred_element_type=jnp.float32) * inv_root
            masked = jnp.where(allowed, logits, -1e+30)
            row_top = lax.optimization_barrier(jnp.max(masked, axis=1, keepdims=True))
            soft = jnp.where(allowed, jnp.exp(masked - row_top), 0.0)
            run_total = lax.optimization_barrier(jnp.sum(soft, axis=1, keepdims=True))
            log_total = row_top + jnp.log(run_total)
            soft_bf = soft.astype(jnp.bfloat16)
            attention = (jnp.dot(soft_bf, v_head, preferred_element_type=jnp.float32) / run_total).astype(jnp.bfloat16)
            row_delta = lax.optimization_barrier(jnp.sum(g_head.astype(jnp.float32) * attention.astype(jnp.float32), axis=1, keepdims=True))
            prob_bf = jnp.where(allowed, jnp.exp(masked - log_total), 0.0).astype(jnp.bfloat16)
            grad_probs = jnp.dot(g_head, v_head.T, preferred_element_type=jnp.float32)
            grad_scores = (prob_bf.astype(jnp.float32) * (grad_probs - row_delta)).astype(jnp.bfloat16)
            grad_query = (jnp.dot(grad_scores, k_head, preferred_element_type=jnp.float32) * inv_root).astype(jnp.bfloat16)
            grad_key = (jnp.dot(grad_scores.T, q_head, preferred_element_type=jnp.float32) * inv_root).astype(jnp.bfloat16)
            grad_value = jnp.dot(prob_bf.T, g_head, preferred_element_type=jnp.float32).astype(jnp.bfloat16)
            return (attention, grad_query, grad_key, grad_value)
        stacks = lax.map(head_pass, (by_head(queries[group_index]), by_head(keys[group_index]), by_head(values[group_index]), by_head(grad_attn)))
        attention = merge_heads(stacks[0])
        layer_term = jnp.dot(attention, w_out, preferred_element_type=jnp.float32).astype(jnp.bfloat16)
        weight_grad = weight_grad + jnp.dot(attention.T, cotangent[group_index], preferred_element_type=jnp.float32)
        outputs.append((layer_term, merge_heads(stacks[1]), merge_heads(stacks[2]), merge_heads(stacks[3])))
    return (jnp.stack([item[0] for item in outputs]), jnp.stack([item[1] for item in outputs]), jnp.stack([item[2] for item in outputs]), jnp.stack([item[3] for item in outputs]), weight_grad)
```

```python
import functools
import math

import jax
import jax.numpy as jnp
from jax import lax
from jax.experimental import pallas as pl
from jax.experimental.pallas import tpu as pltpu
from jax.sharding import PartitionSpec as P

HEAD = 128
FRAME = 512
SIDE = 4
ROWS = 192
LINE = SIDE * ROWS
GROUP = SIDE * LINE
HEADS_HERE = 4
WIDTH = HEADS_HERE * HEAD
RING = 8
FULL = RING * WIDTH
BLOCK = 256
CHUNK = 512
NEG = -1e30
ROOT = 1.0 / math.sqrt(HEAD)
EXP_SCALE = ROOT * math.log2(math.e)
BF = jnp.bfloat16
F32 = jnp.float32

VMEM = pl.BlockSpec(memory_space=pltpu.VMEM)
SMEM = pl.BlockSpec(memory_space=pltpu.SMEM)


def sds(*shape, dtype=BF):
    return jax.ShapeDtypeStruct(shape, dtype)


def call(kernel, meta, args, outs, scratch=(), flops=0, nbytes=0, name=None):
    return pl.pallas_call(
        kernel,
        out_shape=outs,
        in_specs=[SMEM] + [VMEM] * len(args),
        out_specs=[VMEM] * len(outs),
        scratch_shapes=list(scratch),
        compiler_params=pltpu.CompilerParams(vmem_limit_bytes=40 * 1024 * 1024),
        cost_estimate=pl.CostEstimate(flops=flops, bytes_accessed=nbytes, transcendentals=0),
        name=name,
    )(meta, *args)


def nt(a, b):
    return lax.dot_general(a, b, (((1,), (1,)), ((), ())), preferred_element_type=F32)


def nn(a, b):
    return jnp.dot(a, b, preferred_element_type=F32)


def row_at(x, shift):
    return pl.multiple_of(lax.rem(x - shift + SIDE, SIDE) * ROWS, 64)


def line_at(y, shift):
    return pl.multiple_of(lax.rem(y - shift + SIDE, SIDE) * LINE, 256)


def col_at(x, shift):
    return pl.multiple_of(lax.rem(x + shift, SIDE) * HEAD, HEAD)


def bounds(meta, position):
    first = meta[4]
    second = first + meta[5]
    total = second + meta[6]
    in_third = position >= second
    in_second = position >= first
    lo = jnp.where(in_third, second, jnp.where(in_second, first, 0))
    end = jnp.where(in_third, total, jnp.where(in_second, second, first))
    hi = jnp.minimum(end, lo + (lax.shift_right_logical(position - lo, 9) + 1) * FRAME)
    return lo, hi


def to_row(column):
    n = column.shape[0]
    return jnp.transpose(jnp.broadcast_to(column, (n, 128)))[0:1]


def to_column(row):
    n = row.shape[1]
    return jnp.transpose(jnp.broadcast_to(row, (128, n)))[:, 0:1]


def pack_kernel(meta, q, k, v, *outs):
    x = meta[2]
    for d in range(SIDE):
        at = pl.ds(col_at(x, d), HEAD)
        outs[d][0] = q[:, at]
        outs[d][1] = k[:, at]
        outs[d][2] = v[:, at]


def place(x, pieces, target, base=0):
    for d in range(SIDE):
        target[pl.ds(base + row_at(x, d), ROWS), :] = pieces[d]


def gather_lines(x, y, lines, target, slot=None):
    for s in range(SIDE):
        base = line_at(y, s)
        for d in range(SIDE):
            piece = lines[s][d] if slot is None else lines[s][slot, d]
            target[pl.ds(pl.multiple_of(base + row_at(x, d), 64), ROWS), :] = piece


def forward_kernel(meta, q, kv0, kv1, kv2, kv3, out, lse, ks, vs, qs, os, scores):
    y, x = meta[1], meta[2]
    lines = (kv0, kv1, kv2, kv3)
    gather_lines(x, y, lines, ks, 0)
    gather_lines(x, y, lines, vs, 1)
    place(x, q, qs)
    for i in range(LINE // BLOCK):
        rows = pl.ds(i * BLOCK, BLOCK)
        position = y * LINE + i * BLOCK + lax.broadcasted_iota(jnp.int32, (BLOCK, 1), 0)
        lo, hi = bounds(meta, position)
        q_block = qs[rows, :]
        top = jnp.full((BLOCK, 1), NEG, F32)
        for c in range(GROUP // CHUNK):
            at = pl.ds(c * CHUNK, CHUNK)
            s = nt(q_block, ks[at, :]) * EXP_SCALE
            j = c * CHUNK + lax.broadcasted_iota(jnp.int32, (BLOCK, CHUNK), 1)
            s = jnp.where((j >= lo) & (j < hi), s, NEG)
            scores[:, at] = s
            top = jnp.maximum(top, jnp.max(s, axis=1, keepdims=True))
        total = jnp.zeros((BLOCK, 1), F32)
        acc = jnp.zeros((BLOCK, HEAD), F32)
        for c in range(GROUP // CHUNK):
            at = pl.ds(c * CHUNK, CHUNK)
            p = jnp.exp2(scores[:, at] - top)
            total = total + jnp.sum(p, axis=1, keepdims=True)
            acc = acc + nn(p.astype(BF), vs[at, :])
        os[rows, :] = (acc / total).astype(BF)
        lse[0:1, rows] = to_row(top + jnp.log2(total))
    for d in range(SIDE):
        out[d] = os[pl.ds(row_at(x, d), ROWS), :]


def gradient_kernel(meta, *refs):
    blocks, w = refs[:9], refs[9]
    cot, outs, whole = refs[10], refs[11:15], refs[15]
    x, z = meta[2], meta[3]

    def at(shift):
        return pl.ds(pl.multiple_of(lax.rem(z + shift + RING, RING) * WIDTH, WIDTH), WIDTH)

    cot[:, at(0)] = blocks[0][...]
    for s in range(1, 4):
        cot[:, at(-s)] = blocks[2 * s - 1][...]
        cot[:, at(s)] = blocks[2 * s][...]
    cot[: ROWS // 2, at(4)] = blocks[7][...]
    cot[ROWS // 2 :, at(4)] = blocks[8][...]
    whole[...] = nt(cot[...], w[...]).astype(BF)
    for d in range(SIDE):
        outs[d][...] = whole[:, pl.ds(col_at(x, d), HEAD)]


def delta_kernel(meta, attention, lse, g0, g1, g2, g3, grads, stats, os, gs):
    x = meta[2]
    place(x, attention, os)
    pieces = tuple(g[...] for g in (g0, g1, g2, g3))
    place(x, pieces, gs)
    for d in range(SIDE):
        grads[d] = pieces[d]
    stats[...] = jnp.zeros(stats.shape, F32)
    stats[0:1, :] = lse[...]
    for i in range(LINE // BLOCK):
        rows = pl.ds(i * BLOCK, BLOCK)
        product = os[rows, :].astype(F32) * gs[rows, :].astype(F32)
        stats[1:2, rows] = to_row(jnp.sum(product, axis=1, keepdims=True))


def query_kernel(meta, q, grads, stats, kv0, kv1, kv2, kv3, o0, o1, o2, o3, ks, vs, qs, gs, ds):
    y, x = meta[1], meta[2]
    lines = (kv0, kv1, kv2, kv3)
    gather_lines(x, y, lines, ks, 0)
    gather_lines(x, y, lines, vs, 1)
    place(x, q, qs)
    place(x, grads, gs)
    for i in range(LINE // BLOCK):
        rows = pl.ds(i * BLOCK, BLOCK)
        position = y * LINE + i * BLOCK + lax.broadcasted_iota(jnp.int32, (BLOCK, 1), 0)
        lo, hi = bounds(meta, position)
        q_block, g_block = qs[rows, :], gs[rows, :]
        lse = to_column(stats[0:1, rows])
        delta = to_column(stats[1:2, rows])
        acc = jnp.zeros((BLOCK, HEAD), F32)
        for c in range(GROUP // CHUNK):
            at = pl.ds(c * CHUNK, CHUNK)
            k_chunk = ks[at, :]
            s = nt(q_block, k_chunk) * EXP_SCALE - lse
            j = c * CHUNK + lax.broadcasted_iota(jnp.int32, (BLOCK, CHUNK), 1)
            p = jnp.exp2(jnp.where((j >= lo) & (j < hi), s, NEG)).astype(BF)
            dp = nt(g_block, vs[at, :])
            dsc = (p.astype(F32) * (dp - delta)).astype(BF)
            acc = acc + nn(dsc, k_chunk)
        ds[rows, :] = (acc * ROOT).astype(BF)
    for d, out in enumerate((o0, o1, o2, o3)):
        out[...] = ds[pl.ds(row_at(x, d), ROWS), :]


def key_kernel(meta, *refs):
    q_lines, g_lines, stat_lines, kv = refs[0:4], refs[4:8], refs[8:12], refs[12]
    outs = refs[13:17]
    qs, gs, st, ks, vs, dks, dvs = refs[17:]
    y, x = meta[1], meta[2]
    gather_lines(x, y, q_lines, qs)
    gather_lines(x, y, g_lines, gs)
    for s in range(SIDE):
        st[:, pl.ds(line_at(y, s), LINE)] = stat_lines[s][...]
    place(x, tuple(kv[0, d] for d in range(SIDE)), ks)
    place(x, tuple(kv[1, d] for d in range(SIDE)), vs)
    for i in range(LINE // BLOCK):
        rows = pl.ds(i * BLOCK, BLOCK)
        k_block, v_block = ks[rows, :], vs[rows, :]
        j = y * LINE + i * BLOCK + lax.broadcasted_iota(jnp.int32, (BLOCK, CHUNK), 0)
        dk = jnp.zeros((BLOCK, HEAD), F32)
        dv = jnp.zeros((BLOCK, HEAD), F32)
        for c in range(GROUP // CHUNK):
            at = pl.ds(c * CHUNK, CHUNK)
            position = c * CHUNK + lax.broadcasted_iota(jnp.int32, (1, CHUNK), 1)
            lo, hi = bounds(meta, position)
            q_chunk, g_chunk = qs[at, :], gs[at, :]
            s = nt(k_block, q_chunk) * EXP_SCALE - st[0:1, at]
            p = jnp.exp2(jnp.where((j >= lo) & (j < hi), s, NEG)).astype(BF)
            dv = dv + nn(p, g_chunk)
            dp = nt(v_block, g_chunk)
            dsc = (p.astype(F32) * (dp - st[1:2, at])).astype(BF)
            dk = dk + nn(dsc, q_chunk)
        dks[rows, :] = (dk * ROOT).astype(BF)
        dvs[rows, :] = dv.astype(BF)
    for d in range(SIDE):
        at = pl.ds(row_at(x, d), ROWS)
        outs[d][0] = dks[at, :]
        outs[d][1] = dvs[at, :]


def layer_kernel(meta, a0, a1, a2, a3, w, attention, *outs):
    x, z = meta[2], meta[3]
    for d, piece in enumerate((a0, a1, a2, a3)):
        attention[:, pl.ds(col_at(x, d), HEAD)] = piece[...]
    whole = attention[...]
    for j in range(RING):
        at = pl.ds(pl.multiple_of(lax.rem(z + j, RING) * WIDTH, WIDTH), WIDTH)
        outs[j][...] = nn(whole, w[:, at]).astype(BF)


def weight_kernel(meta, attention, cot, keep, send):
    g, y, x = meta[0], meta[1], meta[2]
    turned = jnp.transpose(attention[...].astype(F32)).astype(BF)
    for dx in range(SIDE):
        for dy in range(SIDE):
            index = lax.rem(y + dy, SIDE) * SIDE + lax.rem(x + dx, SIDE)
            at = pl.ds(pl.multiple_of(index * 256, 256), 256)
            term = nn(turned, cot[:, at]).astype(BF)
            low, high = term[:, :128], term[:, 128:]
            keep[dx, dy] = jnp.where(g == 0, low, high)
            send[dx, dy] = jnp.where(g == 0, high, low)


def unpack_kernel(meta, *refs):
    x = meta[2]
    q_parts, kv_parts, (dq, dk, dv) = refs[0:4], refs[4:8], refs[8:11]
    for d in range(SIDE):
        at = pl.ds(col_at(x, d), HEAD)
        dq[:, at] = q_parts[d][...]
        dk[:, at] = kv_parts[d][0]
        dv[:, at] = kv_parts[d][1]


X_SHIFT = {
    d: [(y * SIDE + x, y * SIDE + (x + d) % SIDE) for y in range(SIDE) for x in range(SIDE)]
    for d in range(-3, 4)
}
Y_SHIFT = {
    d: [(y * SIDE + x, ((y + d) % SIDE) * SIDE + x) for y in range(SIDE) for x in range(SIDE)]
    for d in range(-3, 4)
}
Z_SHIFT = {d: [(z, (z + d) % RING) for z in range(RING)] for d in (-1, 1)}


def move_x(a, d):
    return lax.ppermute(a, "ctx", X_SHIFT[d])


def move_y(a, d):
    return lax.ppermute(a, "ctx", Y_SHIFT[d])


def move_z(a, d):
    return lax.ppermute(a, "tp", Z_SHIFT[d])


def sum_all(terms):
    return functools.reduce(lambda a, b: a + b, [t.astype(F32) for t in terms]).astype(BF)


def on_device(queries, keys, values, cotangent, w_out, clip_lengths):
    ctx = lax.axis_index("ctx")
    core = lax.axis_index("dp")
    meta = jnp.concatenate(
        [
            jnp.stack([core, ctx // SIDE, ctx % SIDE, lax.axis_index("tp")]).astype(jnp.int32),
            clip_lengths[0],
            jnp.zeros((1,), jnp.int32),
        ]
    )
    cot_rows = cotangent[0]
    att_cost = dict(flops=4 * LINE * GROUP * HEAD * 2, nbytes=4 * 2**20)
    proj_cost = dict(flops=2 * ROWS * WIDTH * FULL, nbytes=6 * 2**20)

    blocks = [cot_rows]
    ahead, behind = cot_rows, cot_rows
    for step in range(1, 4):
        ahead, behind = move_z(ahead, 1), move_z(behind, -1)
        blocks += [ahead, behind]
    blocks += [move_z(ahead[: ROWS // 2], 1), move_z(behind[ROWS // 2 :], -1)]

    packed = call(
        pack_kernel,
        meta,
        (queries[0], keys[0], values[0]),
        [sds(3, ROWS, HEAD)] * SIDE,
        nbytes=2**21,
        name="pack",
    )
    line = jnp.stack([packed[0]] + [move_x(packed[d], d) for d in range(1, SIDE)], axis=1)
    q_own, kv_own = line[0], line[1:]
    kv = [kv_own] + [move_y(kv_own, d) for d in range(1, SIDE)]
    q_free = lax.optimization_barrier((q_own, kv[1], kv[2], kv[3]))[0]
    q_lines = [q_own] + [move_y(q_free, d) for d in range(1, SIDE)]

    attention, lse = call(
        forward_kernel,
        meta,
        (q_own, *kv),
        [sds(SIDE, ROWS, HEAD), sds(1, LINE, dtype=F32)],
        scratch=[
            pltpu.VMEM((GROUP, HEAD), BF),
            pltpu.VMEM((GROUP, HEAD), BF),
            pltpu.VMEM((LINE, HEAD), BF),
            pltpu.VMEM((LINE, HEAD), BF),
            pltpu.VMEM((BLOCK, GROUP), F32),
        ],
        name="forward",
        **att_cost,
    )
    att_parts = [attention[0]] + [move_x(attention[d], -d) for d in range(1, SIDE)]
    att_rows, *partial = call(
        layer_kernel,
        meta,
        (*att_parts, w_out),
        [sds(ROWS, WIDTH)] * (1 + RING),
        name="layer",
        **proj_cost,
    )
    half = ROWS // 2
    up, down = move_z(partial[4][:half], 1), move_z(partial[4][half:], -1)
    up = jnp.concatenate([partial[3][:half] + up, partial[3][half:]], axis=0)
    down = jnp.concatenate([partial[5][:half], partial[5][half:] + down], axis=0)
    up, down = move_z(up, 1), move_z(down, -1)
    up, down = move_z(partial[2] + up, 1), move_z(partial[6] + down, -1)
    up, down = move_z(partial[1] + up, 1), move_z(partial[7] + down, -1)
    layer_part = sum_all([partial[0], up, down])

    cot_full, *grad_parts = call(
        gradient_kernel,
        meta,
        (*blocks, w_out),
        [sds(ROWS, FULL)] + [sds(ROWS, HEAD)] * SIDE,
        scratch=[pltpu.VMEM((ROWS, WIDTH), BF)],
        name="gradient",
        **proj_cost,
    )
    grad_in = [grad_parts[0]] + [move_x(grad_parts[d], d) for d in range(1, SIDE)]
    grads, stats = call(
        delta_kernel,
        meta,
        (attention, lse, *grad_in),
        [sds(SIDE, ROWS, HEAD), sds(8, LINE, dtype=F32)],
        scratch=[pltpu.VMEM((LINE, HEAD), BF), pltpu.VMEM((LINE, HEAD), BF)],
        nbytes=2**20,
        name="delta",
    )
    grad_lines = [grads] + [move_y(grads, d) for d in range(1, SIDE)]
    stat_lines = [stats] + [move_y(stats, d) for d in range(1, SIDE)]
    dq_parts = call(
        query_kernel,
        meta,
        (q_own, grads, stats, *kv),
        [sds(ROWS, HEAD)] * SIDE,
        scratch=[
            pltpu.VMEM((GROUP, HEAD), BF),
            pltpu.VMEM((GROUP, HEAD), BF),
            pltpu.VMEM((LINE, HEAD), BF),
            pltpu.VMEM((LINE, HEAD), BF),
            pltpu.VMEM((LINE, HEAD), BF),
        ],
        name="query",
        **att_cost,
    )
    dq_back = [dq_parts[0]] + [move_x(dq_parts[d], -d) for d in range(1, SIDE)]
    dkv_parts = call(
        key_kernel,
        meta,
        (*q_lines, *grad_lines, *stat_lines, kv_own),
        [sds(2, ROWS, HEAD)] * SIDE,
        scratch=[
            pltpu.VMEM((GROUP, HEAD), BF),
            pltpu.VMEM((GROUP, HEAD), BF),
            pltpu.VMEM((8, GROUP), F32),
            pltpu.VMEM((LINE, HEAD), BF),
            pltpu.VMEM((LINE, HEAD), BF),
            pltpu.VMEM((LINE, HEAD), BF),
            pltpu.VMEM((LINE, HEAD), BF),
        ],
        name="key",
        **att_cost,
    )
    dkv_back = [dkv_parts[0]] + [move_x(dkv_parts[d], -d) for d in range(1, SIDE)]
    dq, dk, dv = call(
        unpack_kernel,
        meta,
        (*dq_back, *dkv_back),
        [sds(ROWS, WIDTH)] * 3,
        nbytes=2**20,
        name="unpack",
    )

    keep, send = call(
        weight_kernel,
        meta,
        (att_rows, cot_full),
        [sds(SIDE, SIDE, WIDTH, HEAD)] * 2,
        name="weight",
        **proj_cost,
    )
    swap = [(0, 1), (1, 0)]
    term = sum_all([keep, lax.ppermute(send, "dp", swap)])
    term = sum_all([term[0]] + [move_x(term[d], d) for d in range(1, SIDE)])
    term = sum_all([term[0]] + [move_y(term[d], d) for d in range(1, SIDE)])
    other = lax.ppermute(term, "dp", swap)
    first = core == 0
    weight_grad = jnp.concatenate(
        [jnp.where(first, term, other), jnp.where(first, other, term)], axis=1
    ).astype(F32)
    return (layer_part[None], dq[None], dk[None], dv[None], weight_grad)


def solution(mesh):
    in_specs = (
        P("dp", "ctx", "tp"),
        P("dp", "ctx", "tp"),
        P("dp", "ctx", "tp"),
        P("dp", "ctx", "tp"),
        P("tp", None),
        P("dp", None),
    )
    out_specs = (
        P("dp", "ctx", "tp"),
        P("dp", "ctx", "tp"),
        P("dp", "ctx", "tp"),
        P("dp", "ctx", "tp"),
        P("tp", "ctx"),
    )
    return jax.shard_map(
        on_device, mesh=mesh, in_specs=in_specs, out_specs=out_specs, check_vma=False
    )
```

```python
import functools
import math

import jax
import jax.numpy as jnp
from jax import lax
from jax.experimental import pallas as pl
from jax.experimental.pallas import tpu as pltpu
from jax.sharding import PartitionSpec as P

HEAD = 128
FRAME = 512
SIDE = 4
ROWS = 192
LINE = SIDE * ROWS
GROUP = SIDE * LINE
HEADS_HERE = 4
WIDTH = HEADS_HERE * HEAD
RING = 8
FULL = RING * WIDTH
BLOCK = 256
CHUNK = 512
NEG = -1e30
ROOT = 1.0 / math.sqrt(HEAD)
STAT_ROWS = 48
EXP_SCALE = ROOT * math.log2(math.e)
BF = jnp.bfloat16
F32 = jnp.float32

VMEM = pl.BlockSpec(memory_space=pltpu.VMEM)
SMEM = pl.BlockSpec(memory_space=pltpu.SMEM)


def sds(*shape, dtype=BF):
    return jax.ShapeDtypeStruct(shape, dtype)


def call(kernel, meta, args, outs, scratch=(), flops=0, nbytes=0, name=None):
    return pl.pallas_call(
        kernel,
        out_shape=outs,
        in_specs=[SMEM] + [VMEM] * len(args),
        out_specs=[VMEM] * len(outs),
        scratch_shapes=list(scratch),
        compiler_params=pltpu.CompilerParams(vmem_limit_bytes=40 * 1024 * 1024),
        cost_estimate=pl.CostEstimate(flops=flops, bytes_accessed=nbytes, transcendentals=0),
        name=name,
    )(meta, *args)


def nt(a, b):
    return lax.dot_general(a, b, (((1,), (1,)), ((), ())), preferred_element_type=F32)


def nn(a, b):
    return jnp.dot(a, b, preferred_element_type=F32)


def row_at(x, shift):
    return pl.multiple_of(lax.rem(x - shift + SIDE, SIDE) * ROWS, 64)


def line_at(y, shift):
    return pl.multiple_of(lax.rem(y - shift + SIDE, SIDE) * LINE, 256)


def col_at(x, shift):
    return pl.multiple_of(lax.rem(x + shift, SIDE) * HEAD, HEAD)


def bounds(meta, position):
    first = meta[4]
    second = first + meta[5]
    total = second + meta[6]
    in_third = position >= second
    in_second = position >= first
    lo = jnp.where(in_third, second, jnp.where(in_second, first, 0))
    end = jnp.where(in_third, total, jnp.where(in_second, second, first))
    hi = jnp.minimum(end, lo + (lax.shift_right_logical(position - lo, 9) + 1) * FRAME)
    return lo, hi


def to_row(column):
    n = column.shape[0]
    return jnp.transpose(jnp.broadcast_to(column, (n, 128)))[0:1]


def to_column(row):
    n = row.shape[1]
    return jnp.transpose(jnp.broadcast_to(row, (128, n)))[:, 0:1]


def pack_kernel(meta, q, k, v, *outs):
    x = meta[2]
    for d in range(SIDE):
        at = pl.ds(col_at(x, d), HEAD)
        outs[d][0] = q[:, at]
        outs[d][1] = k[:, at]
        outs[d][2] = v[:, at]


def place(x, pieces, target, base=0):
    for d in range(SIDE):
        target[pl.ds(pl.multiple_of(base + row_at(x, d), 64), ROWS), :] = pieces[d]


def gather_lines(x, y, lines, target, slot=None):
    for s in range(SIDE):
        base = line_at(y, s)
        for d in range(SIDE):
            piece = lines[s][d] if slot is None else lines[s][slot, d]
            target[pl.ds(pl.multiple_of(base + row_at(x, d), 64), ROWS), :] = piece


def forward_kernel(meta, kv0, kv1, kv2, kv3, out, lse, ks, vs, qs, os, scores):
    y, x = meta[1], meta[2]
    lines = (kv0, kv1, kv2, kv3)
    gather_lines(x, y, lines, ks, 1)
    gather_lines(x, y, lines, vs, 2)
    place(x, tuple(kv0[0, d] for d in range(SIDE)), qs)
    for i in range(LINE // BLOCK):
        rows = pl.ds(i * BLOCK, BLOCK)
        position = y * LINE + i * BLOCK + lax.broadcasted_iota(jnp.int32, (BLOCK, 1), 0)
        lo, hi = bounds(meta, position)
        q_block = qs[rows, :]
        top = jnp.full((BLOCK, 1), NEG, F32)
        for c in range(GROUP // CHUNK):
            at = pl.ds(c * CHUNK, CHUNK)
            s = nt(q_block, ks[at, :]) * EXP_SCALE
            j = c * CHUNK + lax.broadcasted_iota(jnp.int32, (BLOCK, CHUNK), 1)
            s = jnp.where((j >= lo) & (j < hi), s, NEG)
            scores[:, at] = s
            top = jnp.maximum(top, jnp.max(s, axis=1, keepdims=True))
        total = jnp.zeros((BLOCK, 1), F32)
        acc = jnp.zeros((BLOCK, HEAD), F32)
        for c in range(GROUP // CHUNK):
            at = pl.ds(c * CHUNK, CHUNK)
            p = jnp.exp2(scores[:, at] - top)
            total = total + jnp.sum(p, axis=1, keepdims=True)
            acc = acc + nn(p.astype(BF), vs[at, :])
        os[rows, :] = (acc / total).astype(BF)
        lse[0:1, rows] = to_row(top + jnp.log2(total))
    for d in range(SIDE):
        out[d] = os[pl.ds(row_at(x, d), ROWS), :]


def gradient_kernel(meta, cot, w, o0, o1, o2, o3, whole):
    whole[...] = nt(cot[...], w[...]).astype(BF)
    for d, out in enumerate((o0, o1, o2, o3)):
        out[...] = whole[:, pl.ds(col_at(meta[2], d), HEAD)]


def split3(row):
    high = row.astype(BF).astype(F32)
    middle = (row - high).astype(BF).astype(F32)
    return high, middle, row - high - middle


def delta_kernel(meta, attention, lse, g0, g1, g2, g3, grads, stats, os, gs):
    x = meta[2]
    place(x, attention, os)
    for d, g in enumerate((g0, g1, g2, g3)):
        piece = g[...]
        gs[pl.ds(row_at(x, d), ROWS), :] = piece
        grads[d * ROWS : (d + 1) * ROWS, :] = piece
    stats[...] = jnp.zeros(stats.shape, F32)
    stats[0:1, :] = lse[...]
    for i in range(LINE // BLOCK):
        rows = pl.ds(i * BLOCK, BLOCK)
        product = os[rows, :].astype(F32) * gs[rows, :].astype(F32)
        stats[1:2, rows] = to_row(jnp.sum(product, axis=1, keepdims=True))
    parts = split3(stats[0:1, :]) + split3(stats[1:2, :])
    tiles = [p[:, t * 128 : (t + 1) * 128] for p in parts for t in range(LINE // 128)]
    tiles.append(jnp.zeros((STAT_ROWS - len(tiles), 128), F32))
    grads[LINE:, :] = jnp.concatenate(tiles, axis=0).astype(BF)


def read_stats(line):
    packed = line[LINE:, :].astype(F32)
    n = LINE // 128
    rows = [
        jnp.concatenate([packed[r * n + t : r * n + t + 1] for t in range(n)], axis=1)
        for r in range(6)
    ]
    return rows[0] + (rows[1] + rows[2]), rows[3] + (rows[4] + rows[5])


def query_kernel(meta, grads, stats, kv0, kv1, kv2, kv3, out, ks, vs, qs, gs, ds):
    y, x = meta[1], meta[2]
    lines = (kv0, kv1, kv2, kv3)
    gather_lines(x, y, lines, ks, 1)
    gather_lines(x, y, lines, vs, 2)
    place(x, tuple(kv0[0, d] for d in range(SIDE)), qs)
    place(x, tuple(grads[d * ROWS : (d + 1) * ROWS, :] for d in range(SIDE)), gs)
    for i in range(LINE // BLOCK):
        rows = pl.ds(i * BLOCK, BLOCK)
        position = y * LINE + i * BLOCK + lax.broadcasted_iota(jnp.int32, (BLOCK, 1), 0)
        lo, hi = bounds(meta, position)
        q_block, g_block = qs[rows, :], gs[rows, :]
        lse = to_column(stats[0:1, rows])
        delta = to_column(stats[1:2, rows])
        acc = jnp.zeros((BLOCK, HEAD), F32)
        for c in range(GROUP // CHUNK):
            at = pl.ds(c * CHUNK, CHUNK)
            k_chunk = ks[at, :]
            s = nt(q_block, k_chunk) * EXP_SCALE - lse
            j = c * CHUNK + lax.broadcasted_iota(jnp.int32, (BLOCK, CHUNK), 1)
            p = jnp.exp2(jnp.where((j >= lo) & (j < hi), s, NEG)).astype(BF)
            dp = nt(g_block, vs[at, :])
            dsc = (p.astype(F32) * (dp - delta)).astype(BF)
            acc = acc + nn(dsc, k_chunk)
        ds[rows, :] = (acc * ROOT).astype(BF)
    for d in range(SIDE):
        out[d] = ds[pl.ds(row_at(x, d), ROWS), :]


def key_kernel(meta, kv0, kv1, kv2, kv3, g0, g1, g2, g3, dq, o0, o1, o2, o3, *scratch):
    qs, gs, st, ks, vs, dks, dvs = scratch
    y, x = meta[1], meta[2]
    gather_lines(x, y, (kv0, kv1, kv2, kv3), qs, 0)
    for s, line in enumerate((g0, g1, g2, g3)):
        base = line_at(y, s)
        place(x, tuple(line[d * ROWS : (d + 1) * ROWS, :] for d in range(SIDE)), gs, base)
        lse, delta = read_stats(line)
        st[0:1, pl.ds(base, LINE)] = lse
        st[1:2, pl.ds(base, LINE)] = delta
    place(x, tuple(kv0[1, d] for d in range(SIDE)), ks)
    place(x, tuple(kv0[2, d] for d in range(SIDE)), vs)
    for i in range(LINE // BLOCK):
        rows = pl.ds(i * BLOCK, BLOCK)
        k_block, v_block = ks[rows, :], vs[rows, :]
        j = y * LINE + i * BLOCK + lax.broadcasted_iota(jnp.int32, (BLOCK, CHUNK), 0)
        dk = jnp.zeros((BLOCK, HEAD), F32)
        dv = jnp.zeros((BLOCK, HEAD), F32)
        for c in range(GROUP // CHUNK):
            at = pl.ds(c * CHUNK, CHUNK)
            position = c * CHUNK + lax.broadcasted_iota(jnp.int32, (1, CHUNK), 1)
            lo, hi = bounds(meta, position)
            q_chunk, g_chunk = qs[at, :], gs[at, :]
            s = nt(k_block, q_chunk) * EXP_SCALE - st[0:1, at]
            p = jnp.exp2(jnp.where((j >= lo) & (j < hi), s, NEG)).astype(BF)
            dv = dv + nn(p, g_chunk)
            dp = nt(v_block, g_chunk)
            dsc = (p.astype(F32) * (dp - st[1:2, at])).astype(BF)
            dk = dk + nn(dsc, q_chunk)
        dks[rows, :] = (dk * ROOT).astype(BF)
        dvs[rows, :] = dv.astype(BF)
    for d, out in enumerate((o0, o1, o2, o3)):
        at = pl.ds(row_at(x, d), ROWS)
        out[0] = dq[d]
        out[1] = dks[at, :]
        out[2] = dvs[at, :]


def layer_kernel(meta, a0, a1, a2, a3, w, attention, out):
    for d, piece in enumerate((a0, a1, a2, a3)):
        attention[:, pl.ds(col_at(meta[2], d), HEAD)] = piece[...]
    whole = attention[...]
    for j in range(RING):
        at = pl.ds(j * WIDTH, WIDTH)
        out[:, at] = nn(whole, w[:, at]).astype(BF)


def weight_kernel(meta, attention, cot, keep, send):
    g, y, x = meta[0], meta[1], meta[2]
    turned = jnp.transpose(attention[...].astype(F32)).astype(BF)
    for dx in range(SIDE):
        for dy in range(SIDE):
            index = lax.rem(y + dy, SIDE) * SIDE + lax.rem(x + dx, SIDE)
            at = pl.ds(pl.multiple_of(index * 256, 256), 256)
            term = nn(turned, cot[:, at]).astype(BF)
            low, high = term[:, :128], term[:, 128:]
            keep[dx, dy] = jnp.where(g == 0, low, high)
            send[dx, dy] = jnp.where(g == 0, high, low)


def unpack_kernel(meta, *refs):
    x = meta[2]
    parts, (dq, dk, dv) = refs[0:4], refs[4:7]
    for d in range(SIDE):
        at = pl.ds(col_at(x, d), HEAD)
        dq[:, at] = parts[d][0]
        dk[:, at] = parts[d][1]
        dv[:, at] = parts[d][2]


X_SHIFT = {
    d: [(y * SIDE + x, y * SIDE + (x + d) % SIDE) for y in range(SIDE) for x in range(SIDE)]
    for d in range(-3, 4)
}
Y_SHIFT = {
    d: [(y * SIDE + x, ((y + d) % SIDE) * SIDE + x) for y in range(SIDE) for x in range(SIDE)]
    for d in range(-3, 4)
}


def move_x(a, d):
    return lax.ppermute(a, "ctx", X_SHIFT[d])


def move_y(a, d):
    return lax.ppermute(a, "ctx", Y_SHIFT[d])


def sum_all(terms):
    return functools.reduce(lambda a, b: a + b, [t.astype(F32) for t in terms]).astype(BF)


def on_device(queries, keys, values, cotangent, w_out, clip_lengths):
    ctx = lax.axis_index("ctx")
    core = lax.axis_index("dp")
    meta = jnp.concatenate(
        [
            jnp.stack([core, ctx // SIDE, ctx % SIDE, lax.axis_index("tp")]).astype(jnp.int32),
            clip_lengths[0],
            jnp.zeros((1,), jnp.int32),
        ]
    )
    att_cost = dict(flops=4 * LINE * GROUP * HEAD * 2, nbytes=4 * 2**20)
    proj_cost = dict(flops=2 * ROWS * WIDTH * FULL, nbytes=6 * 2**20)

    cot_full = lax.all_gather(cotangent[0], "tp", axis=1, tiled=True)

    packed = call(
        pack_kernel,
        meta,
        (queries[0], keys[0], values[0]),
        [sds(3, ROWS, HEAD)] * SIDE,
        nbytes=2**21,
        name="pack",
    )
    own = jnp.stack([packed[0]] + [move_x(packed[d], d) for d in range(1, SIDE)], axis=1)
    lines = [own] + [move_y(own, d) for d in range(1, SIDE)]

    attention, lse = call(
        forward_kernel,
        meta,
        lines,
        [sds(SIDE, ROWS, HEAD), sds(1, LINE, dtype=F32)],
        scratch=[
            pltpu.VMEM((GROUP, HEAD), BF),
            pltpu.VMEM((GROUP, HEAD), BF),
            pltpu.VMEM((LINE, HEAD), BF),
            pltpu.VMEM((LINE, HEAD), BF),
            pltpu.VMEM((BLOCK, GROUP), F32),
        ],
        name="forward",
        **att_cost,
    )
    att_parts = [attention[0]] + [move_x(attention[d], -d) for d in range(1, SIDE)]
    att_rows, partial = call(
        layer_kernel,
        meta,
        (*att_parts, w_out),
        [sds(ROWS, WIDTH), sds(ROWS, FULL)],
        name="layer",
        **proj_cost,
    )
    layer_part = lax.psum_scatter(partial, "tp", scatter_dimension=1, tiled=True)

    grad_parts = call(
        gradient_kernel,
        meta,
        (cot_full, w_out),
        [sds(ROWS, HEAD)] * SIDE,
        scratch=[pltpu.VMEM((ROWS, WIDTH), BF)],
        name="gradient",
        **proj_cost,
    )
    grad_in = [grad_parts[0]] + [move_x(grad_parts[d], d) for d in range(1, SIDE)]
    grads, stats = call(
        delta_kernel,
        meta,
        (attention, lse, *grad_in),
        [sds(LINE + STAT_ROWS, HEAD), sds(8, LINE, dtype=F32)],
        scratch=[pltpu.VMEM((LINE, HEAD), BF), pltpu.VMEM((LINE, HEAD), BF)],
        nbytes=2**20,
        name="delta",
    )
    grad_lines = [grads] + [move_y(grads, d) for d in range(1, SIDE)]
    dq = call(
        query_kernel,
        meta,
        (grads, stats, *lines),
        [sds(SIDE, ROWS, HEAD)],
        scratch=[
            pltpu.VMEM((GROUP, HEAD), BF),
            pltpu.VMEM((GROUP, HEAD), BF),
            pltpu.VMEM((LINE, HEAD), BF),
            pltpu.VMEM((LINE, HEAD), BF),
            pltpu.VMEM((LINE, HEAD), BF),
        ],
        name="query",
        **att_cost,
    )[0]
    parts = call(
        key_kernel,
        meta,
        (*lines, *grad_lines, dq),
        [sds(3, ROWS, HEAD)] * SIDE,
        scratch=[
            pltpu.VMEM((GROUP, HEAD), BF),
            pltpu.VMEM((GROUP, HEAD), BF),
            pltpu.VMEM((8, GROUP), F32),
            pltpu.VMEM((LINE, HEAD), BF),
            pltpu.VMEM((LINE, HEAD), BF),
            pltpu.VMEM((LINE, HEAD), BF),
            pltpu.VMEM((LINE, HEAD), BF),
        ],
        name="key",
        **att_cost,
    )
    back = [parts[0]] + [move_x(parts[d], -d) for d in range(1, SIDE)]
    dq, dk, dv = call(
        unpack_kernel, meta, back, [sds(ROWS, WIDTH)] * 3, nbytes=2**20, name="unpack"
    )

    keep, send = call(
        weight_kernel,
        meta,
        (att_rows, cot_full),
        [sds(SIDE, SIDE, WIDTH, HEAD)] * 2,
        name="weight",
        **proj_cost,
    )
    swap = [(0, 1), (1, 0)]
    term = sum_all([keep, lax.ppermute(send, "dp", swap)])
    term = sum_all([term[0]] + [move_x(term[d], d) for d in range(1, SIDE)])
    term = sum_all([term[0]] + [move_y(term[d], d) for d in range(1, SIDE)])
    other = lax.ppermute(term, "dp", swap)
    first = core == 0
    weight_grad = jnp.concatenate(
        [jnp.where(first, term, other), jnp.where(first, other, term)], axis=1
    ).astype(F32)
    return (layer_part[None], dq[None], dk[None], dv[None], weight_grad)


def solution(mesh):
    in_specs = (
        P("dp", "ctx", "tp"),
        P("dp", "ctx", "tp"),
        P("dp", "ctx", "tp"),
        P("dp", "ctx", "tp"),
        P("tp", None),
        P("dp", None),
    )
    out_specs = (
        P("dp", "ctx", "tp"),
        P("dp", "ctx", "tp"),
        P("dp", "ctx", "tp"),
        P("dp", "ctx", "tp"),
        P("tp", "ctx"),
    )
    return jax.shard_map(
        on_device, mesh=mesh, in_specs=in_specs, out_specs=out_specs, check_vma=False
    )
```

```python
import functools
import math

import jax
import jax.numpy as jnp
from jax import lax
from jax.experimental import pallas as pl
from jax.experimental.pallas import tpu as pltpu
from jax.sharding import PartitionSpec as P

HEAD = 128
FRAME = 512
SIDE = 4
ROWS = 192
LINE = SIDE * ROWS
GROUP = SIDE * LINE
HEADS_HERE = 4
WIDTH = HEADS_HERE * HEAD
RING = 8
FULL = RING * WIDTH
BLOCK = 256
CHUNK = 512
FAR = -1e9
ROOT = 1.0 / math.sqrt(HEAD)
STAT_ROWS = 48
EXP_SCALE = ROOT * math.log2(math.e)
BF = jnp.bfloat16
F32 = jnp.float32

VMEM = pl.BlockSpec(memory_space=pltpu.VMEM)
SMEM = pl.BlockSpec(memory_space=pltpu.SMEM)
HBM = pl.BlockSpec(memory_space=pltpu.HBM)


def sds(*shape, dtype=BF):
    return jax.ShapeDtypeStruct(shape, dtype)


def call(kernel, args, outs, clips=None, scratch=(), flops=0, nbytes=0, name=None, specs=None):
    lead = [] if clips is None else [clips]
    return pl.pallas_call(
        kernel,
        out_shape=outs,
        in_specs=[SMEM] * len(lead) + (specs or [VMEM] * len(args)),
        out_specs=[VMEM] * len(outs),
        scratch_shapes=list(scratch),
        compiler_params=pltpu.CompilerParams(vmem_limit_bytes=10 * 2**20),
        cost_estimate=pl.CostEstimate(flops=flops, bytes_accessed=nbytes, transcendentals=0),
        name=name,
    )(*lead, *args)


def place_of():
    ctx = lax.axis_index("ctx")
    return lax.div(ctx, SIDE), lax.rem(ctx, SIDE)


def nt(a, b):
    return lax.dot_general(a, b, (((1,), (1,)), ((), ())), preferred_element_type=F32)


def nn(a, b):
    return jnp.dot(a, b, preferred_element_type=F32)


def row_at(x, shift):
    return pl.multiple_of(lax.rem(x - shift + SIDE, SIDE) * ROWS, 64)


def line_at(y, shift):
    return pl.multiple_of(lax.rem(y - shift + SIDE, SIDE) * LINE, 256)


def col_at(x, shift):
    return pl.multiple_of(lax.rem(x + shift, SIDE) * HEAD, HEAD)


def seats(clips):
    lane = lax.broadcasted_iota(jnp.int32, (1, HEAD), 1)
    clip, frame = lax.shift_right_logical(lane, 3), lax.bitwise_and(lane, 7)
    first = clips[0, 0]
    second = first + clips[0, 1]
    total = second + clips[0, 2]
    start = jnp.where(clip == 0, 0, jnp.where(clip == 1, first, second))
    end = jnp.where(clip == 0, first, jnp.where(clip == 1, second, total))
    end = jnp.where(clip < 3, end, -1)
    start = start + frame * FRAME
    return start, jnp.minimum(end, start + FRAME), end


def key_features(clips, base, rows):
    start, end, _ = seats(clips)
    position = base + lax.broadcasted_iota(jnp.int32, (rows, HEAD), 0)
    return jnp.where((position >= start) & (position < end), 1.0, 0.0).astype(BF)


def query_features(clips, base, rows):
    start, _, end = seats(clips)
    position = base + lax.broadcasted_iota(jnp.int32, (rows, HEAD), 0)
    return jnp.where((position >= start) & (position < end), 0.0, FAR).astype(BF)


def to_row(column):
    n = column.shape[0]
    return jnp.transpose(jnp.broadcast_to(column, (n, 128)))[0:1]


def to_column(row):
    n = row.shape[1]
    return jnp.transpose(jnp.broadcast_to(row, (128, n)))[:, 0:1]


def pack_kernel(q, k, v, o0, o1, o2, o3, sems):
    x = place_of()[1]
    copies = []
    for d, out in enumerate((o0, o1, o2, o3)):
        at = pl.ds(col_at(x, d), HEAD)
        for n, source in enumerate((q, k, v)):
            copies.append(pltpu.make_async_copy(source.at[:, at], out.at[n], sems.at[d, n]))
    for copy in copies:
        copy.start()
    for copy in copies:
        copy.wait()


def place(x, pieces, target, base=0):
    for d in range(SIDE):
        target[pl.ds(pl.multiple_of(base + row_at(x, d), 64), ROWS), :HEAD] = pieces[d]


def gather_lines(x, y, lines, target, slot=None):
    for s in range(SIDE):
        base = line_at(y, s)
        for d in range(SIDE):
            piece = lines[s][d] if slot is None else lines[s][slot, d]
            target[pl.ds(pl.multiple_of(base + row_at(x, d), 64), ROWS), :HEAD] = piece


def forward_kernel(clips, q, kv0, kv1, kv2, kv3, out, lse, ks, vs, qs, os, scores):
    y, x = place_of()
    lines = (kv0, kv1, kv2, kv3)
    gather_lines(x, y, lines, ks, 0)
    gather_lines(x, y, lines, vs, 1)
    place(x, q, qs)
    qs[:, HEAD:] = query_features(clips, y * LINE, LINE)
    ks[:, HEAD:] = key_features(clips, 0, GROUP)
    for i in range(LINE // BLOCK):
        rows = pl.ds(i * BLOCK, BLOCK)
        q_block = qs[rows, :]
        top = jnp.full((BLOCK, 1), -jnp.inf, F32)
        for c in range(GROUP // CHUNK):
            at = pl.ds(c * CHUNK, CHUNK)
            s = nt(q_block, ks[at, :])
            scores[:, at] = s
            top = jnp.maximum(top, jnp.max(s, axis=1, keepdims=True))
        total = jnp.zeros((BLOCK, 1), F32)
        acc = jnp.zeros((BLOCK, HEAD), F32)
        for c in range(GROUP // CHUNK):
            at = pl.ds(c * CHUNK, CHUNK)
            p = jnp.exp2((scores[:, at] - top) * EXP_SCALE)
            total = total + jnp.sum(p, axis=1, keepdims=True)
            acc = acc + nn(p.astype(BF), vs[at, :])
        os[rows, :] = (acc / total).astype(BF)
        lse[0:1, rows] = to_row(top + jnp.log2(total) * (1.0 / EXP_SCALE))
    for d in range(SIDE):
        out[d] = os[pl.ds(row_at(x, d), ROWS), :]


def gradient_kernel(*refs):
    blocks, w, attention, outs, (keep, send, whole, cot) = (
        refs[:9],
        refs[9],
        refs[10],
        refs[11:15],
        refs[15:],
    )
    x = place_of()[1]
    z = lax.axis_index("tp")
    g = lax.axis_index("dp")

    def at(shift):
        return pl.ds(pl.multiple_of(lax.rem(z + shift + RING, RING) * WIDTH, WIDTH), WIDTH)

    cot[:, at(0)] = blocks[0][...]
    for s in range(1, 4):
        cot[:, at(-s)] = blocks[2 * s - 1][...]
        cot[:, at(s)] = blocks[2 * s][...]
    cot[: ROWS // 2, at(4)] = blocks[7][...]
    cot[ROWS // 2 :, at(4)] = blocks[8][...]
    whole[...] = nt(cot[...], w[...]).astype(BF)
    for d, out in enumerate(outs):
        out[0] = whole[:, pl.ds(col_at(x, d), HEAD)]
        out[1] = attention[(SIDE - d) % SIDE]
    for c in range(SIDE * SIDE):
        low, high = cot[:, c * 256 : c * 256 + 128], cot[:, c * 256 + 128 : c * 256 + 256]
        keep[:, c * 128 : (c + 1) * 128] = jnp.where(g == 0, low, high)
        send[:, c * 128 : (c + 1) * 128] = jnp.where(g == 0, high, low)


def split3(row):
    high = row.astype(BF).astype(F32)
    middle = (row - high).astype(BF).astype(F32)
    return high, middle, row - high - middle


def delta_kernel(attention, lse, q, g0, g1, g2, g3, grads, stats, os, gs):
    x = place_of()[1]
    place(x, attention, os)
    for d, g in enumerate((g0, g1, g2, g3)):
        piece = g[0]
        gs[pl.ds(row_at(x, d), ROWS), :] = piece
        grads[d * ROWS : (d + 1) * ROWS, :] = piece
        grads[LINE + d * ROWS : LINE + (d + 1) * ROWS, :] = q[d]
    stats[...] = jnp.zeros(stats.shape, F32)
    stats[0:1, :] = lse[...]
    for i in range(LINE // BLOCK):
        rows = pl.ds(i * BLOCK, BLOCK)
        product = os[rows, :].astype(F32) * gs[rows, :].astype(F32)
        stats[1:2, rows] = to_row(jnp.sum(product, axis=1, keepdims=True))
    parts = split3(stats[0:1, :]) + split3(stats[1:2, :])
    tiles = [p[:, t * 128 : (t + 1) * 128] for p in parts for t in range(LINE // 128)]
    tiles.append(jnp.zeros((STAT_ROWS - len(tiles), 128), F32))
    grads[2 * LINE :, :] = jnp.concatenate(tiles, axis=0).astype(BF)


def read_stats(line):
    packed = line[2 * LINE :, :].astype(F32)
    n = LINE // 128
    rows = [
        jnp.concatenate([packed[r * n + t : r * n + t + 1] for t in range(n)], axis=1)
        for r in range(6)
    ]
    return rows[0] + (rows[1] + rows[2]), rows[3] + (rows[4] + rows[5])


def query_kernel(clips, q, grads, stats, kv0, kv1, kv2, kv3, out, ks, vs, qs, gs, ds):
    y, x = place_of()
    lines = (kv0, kv1, kv2, kv3)
    gather_lines(x, y, lines, ks, 0)
    gather_lines(x, y, lines, vs, 1)
    place(x, q, qs)
    place(x, tuple(grads[d * ROWS : (d + 1) * ROWS, :] for d in range(SIDE)), gs)
    qs[:, HEAD:] = query_features(clips, y * LINE, LINE)
    ks[:, HEAD:] = key_features(clips, 0, GROUP)
    for i in range(LINE // BLOCK):
        rows = pl.ds(i * BLOCK, BLOCK)
        q_block, g_block = qs[rows, :], gs[rows, :]
        lse = to_column(stats[0:1, rows])
        delta = to_column(stats[1:2, rows])
        acc = jnp.zeros((BLOCK, HEAD), F32)
        for c in range(GROUP // CHUNK):
            at = pl.ds(c * CHUNK, CHUNK)
            p = jnp.exp2((nt(q_block, ks[at, :]) - lse) * EXP_SCALE)
            dp = nt(g_block, vs[at, :])
            acc = acc + nn((p * (dp - delta)).astype(BF), ks[at, :HEAD])
        ds[rows, :] = (acc * ROOT).astype(BF)
    for d in range(SIDE):
        out[d] = ds[pl.ds(row_at(x, d), ROWS), :]


def key_kernel(clips, kv0, g0, g1, g2, g3, dq, o0, o1, o2, o3, *scratch):
    qs, gs, st, ks, vs, dks, dvs = scratch
    y, x = place_of()
    for s, line in enumerate((g0, g1, g2, g3)):
        base = line_at(y, s)
        place(x, tuple(line[d * ROWS : (d + 1) * ROWS, :] for d in range(SIDE)), gs, base)
        place(
            x,
            tuple(line[LINE + d * ROWS : LINE + (d + 1) * ROWS, :] for d in range(SIDE)),
            qs,
            base,
        )
        lse, delta = read_stats(line)
        st[0:1, pl.ds(base, LINE)] = lse
        st[1:2, pl.ds(base, LINE)] = delta
    place(x, tuple(kv0[0, d] for d in range(SIDE)), ks)
    place(x, tuple(kv0[1, d] for d in range(SIDE)), vs)
    qs[:, HEAD:] = query_features(clips, 0, GROUP)
    ks[:, HEAD:] = key_features(clips, y * LINE, LINE)
    for i in range(LINE // BLOCK):
        rows = pl.ds(i * BLOCK, BLOCK)
        k_block, v_block = ks[rows, :], vs[rows, :]
        dk = jnp.zeros((BLOCK, HEAD), F32)
        dv = jnp.zeros((BLOCK, HEAD), F32)
        for c in range(GROUP // CHUNK):
            at = pl.ds(c * CHUNK, CHUNK)
            g_chunk = gs[at, :]
            p = jnp.exp2((nt(k_block, qs[at, :]) - st[0:1, at]) * EXP_SCALE)
            dv = dv + nn(p.astype(BF), g_chunk)
            dp = nt(v_block, g_chunk)
            dk = dk + nn((p * (dp - st[1:2, at])).astype(BF), qs[at, :HEAD])
        dks[rows, :] = (dk * ROOT).astype(BF)
        dvs[rows, :] = dv.astype(BF)
    for d, out in enumerate((o0, o1, o2, o3)):
        at = pl.ds(row_at(x, d), ROWS)
        out[0] = dq[d]
        out[1] = dks[at, :]
        out[2] = dvs[at, :]


def layer_kernel(a0, a1, a2, a3, w, attention, out):
    x = place_of()[1]
    for d, piece in enumerate((a0, a1, a2, a3)):
        attention[:, pl.ds(col_at(x, SIDE - d), HEAD)] = piece[1]
    whole = attention[...]
    for j in range(RING):
        at = pl.ds(j * WIDTH, WIDTH)
        out[:, at] = nn(whole, w[:, at]).astype(BF)


def weight_kernel(att, att_other, cot, cot_other, out):
    y, x = place_of()
    both = jnp.concatenate([att[...], att_other[...]], axis=0)
    turned = jnp.transpose(both.astype(F32)).astype(BF)
    for row in range(SIDE):
        at = pl.ds(row * WIDTH, WIDTH)
        term = nn(turned[:, :ROWS], cot[:, at]) + nn(turned[:, ROWS:], cot_other[:, at])
        dy = lax.rem(row - y + SIDE, SIDE)
        for column in range(SIDE):
            dx = lax.rem(column - x + SIDE, SIDE)
            out[dx, dy] = term[:, column * HEAD : (column + 1) * HEAD].astype(BF)


def unpack_kernel(*refs):
    x = place_of()[1]
    parts, (dq, dk, dv) = refs[0:4], refs[4:7]
    for d in range(SIDE):
        at = pl.ds(col_at(x, d), HEAD)
        dq[:, at] = parts[d][0]
        dk[:, at] = parts[d][1]
        dv[:, at] = parts[d][2]


X_SHIFT = {
    d: [(y * SIDE + x, y * SIDE + (x + d) % SIDE) for y in range(SIDE) for x in range(SIDE)]
    for d in range(-3, 4)
}
Y_SHIFT = {
    d: [(y * SIDE + x, ((y + d) % SIDE) * SIDE + x) for y in range(SIDE) for x in range(SIDE)]
    for d in range(-3, 4)
}

Z_SHIFT = {d: [(z, (z + d) % RING) for z in range(RING)] for d in (-1, 1)}


def move_x(a, d):
    return lax.ppermute(a, "ctx", X_SHIFT[d])


def move_y(a, d):
    return lax.ppermute(a, "ctx", Y_SHIFT[d])


def move_z(a, d):
    return lax.ppermute(a, "tp", Z_SHIFT[d])


def sum_all(terms):
    return functools.reduce(lambda a, b: a + b, [t.astype(F32) for t in terms]).astype(BF)


def after(a, *others):
    return lax.optimization_barrier((a, *others))[0]


def on_device(queries, keys, values, cotangent, w_out, clip_lengths):
    core = lax.axis_index("dp")
    swap = [(0, 1), (1, 0)]
    att_cost = dict(flops=4 * LINE * GROUP * HEAD * 2, nbytes=4 * 2**20)
    proj_cost = dict(flops=2 * ROWS * WIDTH * FULL, nbytes=6 * 2**20)

    cot = cotangent[0]
    ahead1, behind1 = move_z(cot, 1), move_z(cot, -1)
    packed = call(
        pack_kernel,
        (queries[0], keys[0], values[0]),
        [sds(3, ROWS, HEAD)] * SIDE,
        scratch=[pltpu.SemaphoreType.DMA((SIDE, 3))],
        nbytes=2**21,
        name="pack",
        specs=[HBM] * 3,
    )
    ahead2, behind2 = move_z(ahead1, 1), move_z(behind1, -1)
    line = jnp.stack([packed[0]] + [move_x(packed[d], d) for d in range(1, SIDE)], axis=1)
    q_own, kv_own = line[0], line[1:]
    kv_own = after(kv_own, ahead2, behind2)
    kv = [kv_own] + [move_y(kv_own, d) for d in range(1, SIDE)]
    ahead3, behind3 = move_z(ahead2, 1), move_z(behind2, -1)
    ahead4 = move_z(ahead3[: ROWS // 2], 1)
    behind4 = move_z(behind3[ROWS // 2 :], -1)
    blocks = [cot, ahead1, behind1, ahead2, behind2, ahead3, behind3, ahead4, behind4]
    kv, _, _ = lax.optimization_barrier((kv, ahead4, behind4))

    attention, lse = call(
        forward_kernel,
        (q_own, *kv),
        [sds(SIDE, ROWS, HEAD), sds(1, LINE, dtype=F32)],
        clips=clip_lengths,
        scratch=[
            pltpu.VMEM((GROUP, 2 * HEAD), BF),
            pltpu.VMEM((GROUP, HEAD), BF),
            pltpu.VMEM((LINE, 2 * HEAD), BF),
            pltpu.VMEM((LINE, HEAD), BF),
            pltpu.VMEM((BLOCK, GROUP), F32),
        ],
        name="forward",
        **att_cost,
    )

    *grad_parts, cot_keep, cot_send = call(
        gradient_kernel,
        (*blocks, w_out, attention),
        [sds(2, ROWS, HEAD)] * SIDE + [sds(ROWS, FULL // 2)] * 2,
        scratch=[pltpu.VMEM((ROWS, WIDTH), BF), pltpu.VMEM((ROWS, FULL), BF)],
        name="gradient",
        **proj_cost,
    )
    mixed = [grad_parts[0]] + [move_x(grad_parts[d], d) for d in range(1, SIDE)]
    att_rows, partial = call(
        layer_kernel,
        (*mixed, w_out),
        [sds(ROWS, WIDTH), sds(ROWS, FULL)],
        name="layer",
        **proj_cost,
    )
    layer_part = lax.psum_scatter(partial, "tp", scatter_dimension=1, tiled=True)
    grads, stats = call(
        delta_kernel,
        (attention, lse, q_own, *mixed),
        [sds(2 * LINE + STAT_ROWS, HEAD), sds(8, LINE, dtype=F32)],
        scratch=[pltpu.VMEM((LINE, HEAD), BF), pltpu.VMEM((LINE, HEAD), BF)],
        nbytes=2**20,
        name="delta",
    )
    grad_lines = [grads] + [move_y(grads, d) for d in range(1, SIDE)]

    att_swap, cot_swap = after(att_rows, grads), after(cot_send, grads)
    term = call(
        weight_kernel,
        (
            after(att_rows, partial),
            lax.ppermute(att_swap, "dp", swap),
            cot_keep,
            lax.ppermute(cot_swap, "dp", swap),
        ),
        [sds(SIDE, SIDE, WIDTH, HEAD)],
        name="weight",
        **proj_cost,
    )[0]
    term_parts = [term[0]] + [move_x(term[d], d) for d in range(1, SIDE)]
    dq = call(
        query_kernel,
        (q_own, grads, stats, *kv),
        [sds(SIDE, ROWS, HEAD)],
        clips=clip_lengths,
        scratch=[
            pltpu.VMEM((GROUP, 2 * HEAD), BF),
            pltpu.VMEM((GROUP, HEAD), BF),
            pltpu.VMEM((LINE, 2 * HEAD), BF),
            pltpu.VMEM((LINE, HEAD), BF),
            pltpu.VMEM((LINE, HEAD), BF),
        ],
        name="query",
        **att_cost,
    )[0]
    parts = call(
        key_kernel,
        (kv_own, *grad_lines, dq),
        [sds(3, ROWS, HEAD)] * SIDE,
        clips=clip_lengths,
        scratch=[
            pltpu.VMEM((GROUP, 2 * HEAD), BF),
            pltpu.VMEM((GROUP, HEAD), BF),
            pltpu.VMEM((8, GROUP), F32),
            pltpu.VMEM((LINE, 2 * HEAD), BF),
            pltpu.VMEM((LINE, HEAD), BF),
            pltpu.VMEM((LINE, HEAD), BF),
            pltpu.VMEM((LINE, HEAD), BF),
        ],
        name="key",
        **att_cost,
    )
    term_parts = after(term_parts, parts)
    weight_part = sum_all(term_parts)
    weight_part = sum_all(
        [weight_part[0]] + [move_y(weight_part[d], d) for d in range(1, SIDE)]
    )
    other = lax.ppermute(weight_part, "dp", swap)
    first = core == 0
    weight_grad = jnp.concatenate(
        [jnp.where(first, weight_part, other), jnp.where(first, other, weight_part)], axis=1
    ).astype(F32)

    back = [parts[0]] + [move_x(parts[d], -d) for d in range(1, SIDE)]
    dq, dk, dv = call(unpack_kernel, back, [sds(ROWS, WIDTH)] * 3, nbytes=2**20, name="unpack")
    return (layer_part[None], dq[None], dk[None], dv[None], weight_grad)


def solution(mesh):
    in_specs = (
        P("dp", "ctx", "tp"),
        P("dp", "ctx", "tp"),
        P("dp", "ctx", "tp"),
        P("dp", "ctx", "tp"),
        P("tp", None),
        P("dp", None),
    )
    out_specs = (
        P("dp", "ctx", "tp"),
        P("dp", "ctx", "tp"),
        P("dp", "ctx", "tp"),
        P("dp", "ctx", "tp"),
        P("tp", "ctx"),
    )
    return jax.shard_map(
        on_device, mesh=mesh, in_specs=in_specs, out_specs=out_specs, check_vma=False
    )
```

```python
import functools
import math

import jax
import jax.numpy as jnp
from jax import lax
from jax.experimental import pallas as pl
from jax.experimental.pallas import tpu as pltpu
from jax.sharding import PartitionSpec as P

HEAD = 128
FRAME = 512
SIDE = 4
ROWS = 192
LINE = SIDE * ROWS
GROUP = SIDE * LINE
HEADS_HERE = 4
WIDTH = HEADS_HERE * HEAD
RING = 8
FULL = RING * WIDTH
BLOCK = 256
CHUNK = 512
WIDE = 768
SLIM = 256
FAR = -1e9
ROOT = 1.0 / math.sqrt(HEAD)
STAT_ROWS = 48
EXP_SCALE = ROOT * math.log2(math.e)
BF = jnp.bfloat16
F32 = jnp.float32

VMEM = pl.BlockSpec(memory_space=pltpu.VMEM)
SMEM = pl.BlockSpec(memory_space=pltpu.SMEM)


def sds(*shape, dtype=BF):
    return jax.ShapeDtypeStruct(shape, dtype)


def call(kernel, args, outs, clips=None, scratch=(), micros=1, name=None, room=6):
    lead = [] if clips is None else [clips]
    return pl.pallas_call(
        kernel,
        out_shape=outs,
        in_specs=[SMEM] * len(lead) + [VMEM] * len(args),
        out_specs=[VMEM] * len(outs),
        scratch_shapes=list(scratch),
        compiler_params=pltpu.CompilerParams(vmem_limit_bytes=room * 2**20),
        cost_estimate=pl.CostEstimate(
            flops=int(micros * 1.15e9), bytes_accessed=2**20, transcendentals=0
        ),
        name=name,
    )(*lead, *args)


def place_of():
    ctx = lax.axis_index("ctx")
    return lax.div(ctx, SIDE), lax.rem(ctx, SIDE)


def nt(a, b):
    return lax.dot_general(a, b, (((1,), (1,)), ((), ())), preferred_element_type=F32)


def nn(a, b):
    return jnp.dot(a, b, preferred_element_type=F32)


def row_at(x, shift):
    return pl.multiple_of(lax.rem(x - shift + SIDE, SIDE) * ROWS, 64)


def line_at(y, shift):
    return pl.multiple_of(lax.rem(y - shift + SIDE, SIDE) * LINE, 256)


def col_at(x, shift):
    return pl.multiple_of(lax.rem(x + shift, SIDE) * HEAD, HEAD)


def seats(clips):
    lane = lax.broadcasted_iota(jnp.int32, (1, HEAD), 1)
    clip, frame = lax.shift_right_logical(lane, 3), lax.bitwise_and(lane, 7)
    first = clips[0, 0]
    second = first + clips[0, 1]
    total = second + clips[0, 2]
    start = jnp.where(clip == 0, 0, jnp.where(clip == 1, first, second))
    end = jnp.where(clip == 0, first, jnp.where(clip == 1, second, total))
    end = jnp.where(clip < 3, end, -1)
    start = start + frame * FRAME
    return start, jnp.minimum(end, start + FRAME), end


def key_features(clips, base, rows):
    start, end, _ = seats(clips)
    position = base + lax.broadcasted_iota(jnp.int32, (rows, HEAD), 0)
    return jnp.where((position >= start) & (position < end), 1.0, 0.0).astype(BF)


def query_features(clips, base, rows):
    start, _, end = seats(clips)
    position = base + lax.broadcasted_iota(jnp.int32, (rows, HEAD), 0)
    return jnp.where((position >= start) & (position < end), 0.0, FAR).astype(BF)


def to_row(column):
    n = column.shape[0]
    return jnp.transpose(jnp.broadcast_to(column, (n, 128)))[0:1]


def to_column(row):
    n = row.shape[1]
    return jnp.transpose(jnp.broadcast_to(row, (128, n)))[:, 0:1]


def place(x, pieces, target, base=0):
    for d in range(SIDE):
        target[pl.ds(pl.multiple_of(base + row_at(x, d), 64), ROWS), :HEAD] = pieces[d]


def gather_lines(x, y, lines, target, slot=None):
    for s in range(SIDE):
        base = line_at(y, s)
        for d in range(SIDE):
            piece = lines[s][d] if slot is None else lines[s][slot, d]
            target[pl.ds(pl.multiple_of(base + row_at(x, d), 64), ROWS), :HEAD] = piece


def forward_kernel(clips, q, kv0, kv1, kv2, kv3, out, lse, ks, vs, qs, os, scores):
    y, x = place_of()
    lines = (kv0, kv1, kv2, kv3)
    gather_lines(x, y, lines, ks, 0)
    gather_lines(x, y, lines, vs, 1)
    place(x, q, qs)
    qs[:, HEAD:] = query_features(clips, y * LINE, LINE)
    ks[:, HEAD:] = key_features(clips, 0, GROUP)
    for i in range(LINE // BLOCK):
        rows = pl.ds(i * BLOCK, BLOCK)
        q_block = qs[rows, :]
        top = jnp.full((BLOCK, 1), -jnp.inf, F32)
        for c in range(GROUP // CHUNK):
            at = pl.ds(c * CHUNK, CHUNK)
            s = nt(q_block, ks[at, :])
            scores[:, at] = s
            top = jnp.maximum(top, jnp.max(s, axis=1, keepdims=True))
        total = jnp.zeros((BLOCK, 1), F32)
        acc = jnp.zeros((BLOCK, HEAD), F32)
        for c in range(GROUP // CHUNK):
            at = pl.ds(c * CHUNK, CHUNK)
            p = jnp.exp2((scores[:, at] - top) * EXP_SCALE)
            total = total + jnp.sum(p, axis=1, keepdims=True)
            acc = acc + nn(p.astype(BF), vs[at, :])
        os[rows, :] = (acc / total).astype(BF)
        lse[0:1, rows] = to_row(top + jnp.log2(total) * (1.0 / EXP_SCALE))
    for d in range(SIDE):
        out[d] = os[pl.ds(row_at(x, d), ROWS), :]


def gradient_kernel(*refs):
    blocks, w, attention, outs, (keep, send, whole, cot) = (
        refs[:8],
        refs[8],
        refs[9],
        refs[10:14],
        refs[14:],
    )
    x = place_of()[1]
    z = lax.axis_index("tp")
    g = lax.axis_index("dp")

    def at(shift):
        return pl.ds(pl.multiple_of(lax.rem(z + shift + RING, RING) * WIDTH, WIDTH), WIDTH)

    cot[:, at(0)] = blocks[0][...]
    for s in range(1, 4):
        cot[:, at(-s)] = blocks[2 * s - 1][...]
        cot[:, at(s)] = blocks[2 * s][...]
    cot[:, at(-4)] = blocks[7][...]
    whole[...] = nt(cot[...], w[...]).astype(BF)
    for d, out in enumerate(outs):
        out[0] = whole[:, pl.ds(col_at(x, d), HEAD)]
        out[1] = attention[(SIDE - d) % SIDE]
    for c in range(SIDE * SIDE):
        low, high = cot[:, c * 256 : c * 256 + 128], cot[:, c * 256 + 128 : c * 256 + 256]
        keep[:, c * 128 : (c + 1) * 128] = jnp.where(g == 0, low, high)
        send[:, c * 128 : (c + 1) * 128] = jnp.where(g == 0, high, low)


def split3(row):
    high = row.astype(BF).astype(F32)
    middle = (row - high).astype(BF).astype(F32)
    return high, middle, row - high - middle


def delta_kernel(attention, lse, q, g0, g1, g2, g3, grads, stats, os, gs):
    x = place_of()[1]
    place(x, attention, os)
    for d, g in enumerate((g0, g1, g2, g3)):
        piece = g[0]
        gs[pl.ds(row_at(x, d), ROWS), :] = piece
        grads[d * ROWS : (d + 1) * ROWS, :] = piece
        grads[LINE + d * ROWS : LINE + (d + 1) * ROWS, :] = q[d]
    stats[...] = jnp.zeros(stats.shape, F32)
    stats[0:1, :] = lse[...]
    for i in range(LINE // BLOCK):
        rows = pl.ds(i * BLOCK, BLOCK)
        product = os[rows, :].astype(F32) * gs[rows, :].astype(F32)
        stats[1:2, rows] = to_row(jnp.sum(product, axis=1, keepdims=True))
    parts = split3(stats[0:1, :]) + split3(stats[1:2, :])
    tiles = [p[:, t * 128 : (t + 1) * 128] for p in parts for t in range(LINE // 128)]
    tiles.append(jnp.zeros((STAT_ROWS - len(tiles), 128), F32))
    grads[2 * LINE :, :] = jnp.concatenate(tiles, axis=0).astype(BF)


def read_stats(line):
    packed = line[2 * LINE :, :].astype(F32)
    n = LINE // 128
    rows = [
        jnp.concatenate([packed[r * n + t : r * n + t + 1] for t in range(n)], axis=1)
        for r in range(6)
    ]
    return rows[0] + (rows[1] + rows[2]), rows[3] + (rows[4] + rows[5])


def query_kernel(clips, q, grads, stats, kv0, kv1, kv2, kv3, out, ks, vs, qs, gs, ds):
    y, x = place_of()
    lines = (kv0, kv1, kv2, kv3)
    gather_lines(x, y, lines, ks, 0)
    gather_lines(x, y, lines, vs, 1)
    place(x, q, qs)
    place(x, tuple(grads[d * ROWS : (d + 1) * ROWS, :] for d in range(SIDE)), gs)
    qs[:, HEAD:] = query_features(clips, y * LINE, LINE)
    ks[:, HEAD:] = key_features(clips, 0, GROUP)
    for i in range(LINE // WIDE):
        rows = pl.ds(i * WIDE, WIDE)
        q_block, g_block = qs[rows, :], gs[rows, :]
        lse = to_column(stats[0:1, rows])
        delta = to_column(stats[1:2, rows])
        acc = jnp.zeros((WIDE, HEAD), F32)
        for c in range(GROUP // SLIM):
            at = pl.ds(c * SLIM, SLIM)
            p = jnp.exp2((nt(q_block, ks[at, :]) - lse) * EXP_SCALE)
            dp = nt(g_block, vs[at, :])
            acc = acc + nn((p * (dp - delta)).astype(BF), ks[at, :HEAD])
        ds[rows, :] = (acc * ROOT).astype(BF)
    for d in range(SIDE):
        out[d] = ds[pl.ds(row_at(x, d), ROWS), :]


def key_kernel(clips, kv0, g0, g1, g2, g3, dq, o0, o1, o2, o3, *scratch):
    qs, gs, st, ks, vs, dks, dvs = scratch
    y, x = place_of()
    for s, line in enumerate((g0, g1, g2, g3)):
        base = line_at(y, s)
        place(x, tuple(line[d * ROWS : (d + 1) * ROWS, :] for d in range(SIDE)), gs, base)
        place(
            x,
            tuple(line[LINE + d * ROWS : LINE + (d + 1) * ROWS, :] for d in range(SIDE)),
            qs,
            base,
        )
        lse, delta = read_stats(line)
        st[0:1, pl.ds(base, LINE)] = lse
        st[1:2, pl.ds(base, LINE)] = delta
    place(x, tuple(kv0[0, d] for d in range(SIDE)), ks)
    place(x, tuple(kv0[1, d] for d in range(SIDE)), vs)
    qs[:, HEAD:] = query_features(clips, 0, GROUP)
    ks[:, HEAD:] = key_features(clips, y * LINE, LINE)
    for i in range(LINE // WIDE):
        rows = pl.ds(i * WIDE, WIDE)
        k_block, v_block = ks[rows, :], vs[rows, :]
        dk = jnp.zeros((WIDE, HEAD), F32)
        dv = jnp.zeros((WIDE, HEAD), F32)
        for c in range(GROUP // SLIM):
            at = pl.ds(c * SLIM, SLIM)
            g_chunk = gs[at, :]
            p = jnp.exp2((nt(k_block, qs[at, :]) - st[0:1, at]) * EXP_SCALE)
            dv = dv + nn(p.astype(BF), g_chunk)
            dp = nt(v_block, g_chunk)
            dk = dk + nn((p * (dp - st[1:2, at])).astype(BF), qs[at, :HEAD])
        dks[rows, :] = (dk * ROOT).astype(BF)
        dvs[rows, :] = dv.astype(BF)
    for d, out in enumerate((o0, o1, o2, o3)):
        at = pl.ds(row_at(x, d), ROWS)
        out[0] = dq[d]
        out[1] = dks[at, :]
        out[2] = dvs[at, :]


def layer_kernel(a0, a1, a2, a3, w, cot, out, mine, attention):
    x = place_of()[1]
    for d, piece in enumerate((a0, a1, a2, a3)):
        attention[:, pl.ds(col_at(x, SIDE - d), HEAD)] = piece[1]
    whole = attention[...]
    mine[:, : FULL // 2] = cot[...]
    mine[:, FULL // 2 :] = whole
    for j in range(RING):
        at = pl.ds(j * WIDTH, WIDTH)
        out[:, at] = nn(whole, w[:, at]).astype(BF)


def weight_kernel(mine, other, cot, out):
    y, x = place_of()
    both = jnp.concatenate([mine[:, FULL // 2 :], other[:, FULL // 2 :]], axis=0)
    turned = jnp.transpose(both.astype(F32)).astype(BF)
    for row in range(SIDE):
        at = pl.ds(row * WIDTH, WIDTH)
        term = nn(turned[:, :ROWS], cot[:, at]) + nn(turned[:, ROWS:], other[:, at])
        dy = lax.rem(row - y + SIDE, SIDE)
        for column in range(SIDE):
            dx = lax.rem(column - x + SIDE, SIDE)
            out[dx, dy] = term[:, column * HEAD : (column + 1) * HEAD].astype(BF)


def unpack_kernel(*refs):
    x = place_of()[1]
    parts, (dq, dk, dv) = refs[0:4], refs[4:7]
    for d in range(SIDE):
        at = pl.ds(col_at(x, d), HEAD)
        dq[:, at] = parts[d][0]
        dk[:, at] = parts[d][1]
        dv[:, at] = parts[d][2]


X_SHIFT = {
    d: [(y * SIDE + x, y * SIDE + (x + d) % SIDE) for y in range(SIDE) for x in range(SIDE)]
    for d in range(-3, 4)
}
Y_SHIFT = {
    d: [(y * SIDE + x, ((y + d) % SIDE) * SIDE + x) for y in range(SIDE) for x in range(SIDE)]
    for d in range(-3, 4)
}

Z_SHIFT = {d: [(z, (z + d) % RING) for z in range(RING)] for d in (-1, 1)}


def move_x(a, d):
    return lax.ppermute(a, "ctx", X_SHIFT[d])


def move_y(a, d):
    return lax.ppermute(a, "ctx", Y_SHIFT[d])


def move_z(a, d):
    return lax.ppermute(a, "tp", Z_SHIFT[d])


def sum_all(terms):
    return functools.reduce(lambda a, b: a + b, [t.astype(F32) for t in terms]).astype(BF)


def after(a, *others):
    return lax.optimization_barrier((a, *others))[0]


def on_device(queries, keys, values, cotangent, w_out, clip_lengths):
    core = lax.axis_index("dp")
    swap = [(0, 1), (1, 0)]

    cot = cotangent[0]
    ahead1, behind1 = move_z(cot, 1), move_z(cot, -1)
    x = place_of()[1]
    packed = [
        jnp.stack(
            [
                lax.dynamic_slice(a[0], (0, lax.rem(x + d, SIDE) * HEAD), (ROWS, HEAD))
                for a in (queries, keys, values)
            ]
        )
        for d in range(SIDE)
    ]
    ahead2, behind2 = move_z(ahead1, 1), move_z(behind1, -1)
    line = jnp.stack([packed[0]] + [move_x(packed[d], d) for d in range(1, SIDE)], axis=1)
    q_own, kv_own = line[0], line[1:]
    kv = [kv_own] + [move_y(kv_own, d) for d in range(1, SIDE)]
    ahead3, behind3 = move_z(ahead2, 1), move_z(behind2, -1)
    ahead4 = move_z(ahead3, 1)
    blocks = [cot, ahead1, behind1, ahead2, behind2, ahead3, behind3, ahead4]
    kv = after(kv, ahead4)

    attention, lse = call(
        forward_kernel,
        (q_own, *kv),
        [sds(SIDE, ROWS, HEAD), sds(1, LINE, dtype=F32)],
        clips=clip_lengths,
        scratch=[
            pltpu.VMEM((GROUP, 2 * HEAD), BF),
            pltpu.VMEM((GROUP, HEAD), BF),
            pltpu.VMEM((LINE, 2 * HEAD), BF),
            pltpu.VMEM((LINE, HEAD), BF),
            pltpu.VMEM((BLOCK, GROUP), F32),
        ],
        name="forward",
        micros=5,
        room=9,
    )

    *grad_parts, cot_keep, cot_send = call(
        gradient_kernel,
        (*blocks, w_out, attention),
        [sds(2, ROWS, HEAD)] * SIDE + [sds(ROWS, FULL // 2)] * 2,
        scratch=[pltpu.VMEM((ROWS, WIDTH), BF), pltpu.VMEM((ROWS, FULL), BF)],
        name="gradient",
        micros=2,
    )
    mixed = [grad_parts[0]] + [move_x(grad_parts[d], d) for d in range(1, SIDE)]
    grads, stats = call(
        delta_kernel,
        (attention, lse, q_own, *mixed),
        [sds(2 * LINE + STAT_ROWS, HEAD), sds(8, LINE, dtype=F32)],
        scratch=[pltpu.VMEM((LINE, HEAD), BF), pltpu.VMEM((LINE, HEAD), BF)],
        name="delta",
    )
    grad_lines = [grads] + [move_y(grads, d) for d in range(1, SIDE)]
    partial, mine = call(
        layer_kernel,
        (*mixed, w_out, cot_send),
        [sds(ROWS, FULL), sds(ROWS, FULL // 2 + WIDTH)],
        scratch=[pltpu.VMEM((ROWS, WIDTH), BF)],
        name="layer",
        micros=2,
    )
    layer_part = lax.psum_scatter(partial, "tp", scatter_dimension=1, tiled=True)

    term = call(
        weight_kernel,
        (after(mine, grads), lax.ppermute(mine, "dp", swap), cot_keep),
        [sds(SIDE, SIDE, WIDTH, HEAD)],
        name="weight",
        micros=2,
    )[0]
    dq = call(
        query_kernel,
        (q_own, grads, after(stats, term), *kv),
        [sds(SIDE, ROWS, HEAD)],
        clips=clip_lengths,
        scratch=[
            pltpu.VMEM((GROUP, 2 * HEAD), BF),
            pltpu.VMEM((GROUP, HEAD), BF),
            pltpu.VMEM((LINE, 2 * HEAD), BF),
            pltpu.VMEM((LINE, HEAD), BF),
            pltpu.VMEM((LINE, HEAD), BF),
        ],
        name="query",
        micros=5,
        room=11,
    )[0]
    up, down = move_x(term[2, :2], 1), move_x(term[2, 2:], -1)
    kv_key = after(kv_own, up, down)
    up = jnp.concatenate([term[1, :2] + up, term[1, 2:]], axis=0)
    down = jnp.concatenate([term[3, :2], term[3, 2:] + down], axis=0)
    term_parts = [term[0], move_x(up, 1), move_x(down, -1)]
    parts = call(
        key_kernel,
        (kv_key, *grad_lines, dq),
        [sds(3, ROWS, HEAD)] * SIDE,
        clips=clip_lengths,
        scratch=[
            pltpu.VMEM((GROUP, 2 * HEAD), BF),
            pltpu.VMEM((GROUP, HEAD), BF),
            pltpu.VMEM((8, GROUP), F32),
            pltpu.VMEM((LINE, 2 * HEAD), BF),
            pltpu.VMEM((LINE, HEAD), BF),
            pltpu.VMEM((LINE, HEAD), BF),
            pltpu.VMEM((LINE, HEAD), BF),
        ],
        name="key",
        micros=24,
        room=11,
    )
    term_parts = after(term_parts, parts)
    weight_part = sum_all(term_parts)
    weight_part = sum_all(
        [weight_part[0]] + [move_y(weight_part[d], d) for d in range(1, SIDE)]
    )
    other = lax.ppermute(weight_part, "dp", swap)
    first = core == 0
    weight_grad = jnp.concatenate(
        [jnp.where(first, weight_part, other), jnp.where(first, other, weight_part)], axis=1
    ).astype(F32)

    back = [parts[0]] + [move_x(parts[d], -d) for d in range(1, SIDE)]
    dq, dk, dv = call(unpack_kernel, back, [sds(ROWS, WIDTH)] * 3, name="unpack")
    return (layer_part[None], dq[None], dk[None], dv[None], weight_grad)


def solution(mesh):
    in_specs = (
        P("dp", "ctx", "tp"),
        P("dp", "ctx", "tp"),
        P("dp", "ctx", "tp"),
        P("dp", "ctx", "tp"),
        P("tp", None),
        P("dp", None),
    )
    out_specs = (
        P("dp", "ctx", "tp"),
        P("dp", "ctx", "tp"),
        P("dp", "ctx", "tp"),
        P("dp", "ctx", "tp"),
        P("tp", "ctx"),
    )
    return jax.shard_map(
        on_device, mesh=mesh, in_specs=in_specs, out_specs=out_specs, check_vma=False
    )
```

```python
import functools
import math

import jax
import jax.numpy as jnp
from jax import lax
from jax.experimental import pallas as pl
from jax.experimental.pallas import tpu as pltpu
from jax.sharding import PartitionSpec as P

HEAD = 128
FRAME = 512
SIDE = 4
ROWS = 192
LINE = SIDE * ROWS
GROUP = SIDE * LINE
HEADS_HERE = 4
WIDTH = HEADS_HERE * HEAD
RING = 8
FULL = RING * WIDTH
BLOCK = 256
CHUNK = 512
WIDE = 768
SLIM = 256
FAR = -1e9
ROOT = 1.0 / math.sqrt(HEAD)
STAT_ROWS = 48
EXP_SCALE = ROOT * math.log2(math.e)
BF = jnp.bfloat16
F32 = jnp.float32

VMEM = pl.BlockSpec(memory_space=pltpu.VMEM)
SMEM = pl.BlockSpec(memory_space=pltpu.SMEM)


def sds(*shape, dtype=BF):
    return jax.ShapeDtypeStruct(shape, dtype)


def call(kernel, args, outs, clips=None, scratch=(), micros=1, name=None, room=5):
    lead = [] if clips is None else [clips]
    return pl.pallas_call(
        kernel,
        out_shape=outs,
        in_specs=[SMEM] * len(lead) + [VMEM] * len(args),
        out_specs=[VMEM] * len(outs),
        scratch_shapes=list(scratch),
        compiler_params=pltpu.CompilerParams(vmem_limit_bytes=room * 2**20),
        cost_estimate=pl.CostEstimate(
            flops=int(micros * 1.15e9), bytes_accessed=2**20, transcendentals=0
        ),
        name=name,
    )(*lead, *args)


def place_of():
    ctx = lax.axis_index("ctx")
    return lax.div(ctx, SIDE), lax.rem(ctx, SIDE)


def nt(a, b):
    return lax.dot_general(a, b, (((1,), (1,)), ((), ())), preferred_element_type=F32)


def nn(a, b):
    return jnp.dot(a, b, preferred_element_type=F32)


def row_at(x, shift):
    return pl.multiple_of(lax.rem(x - shift + SIDE, SIDE) * ROWS, 64)


def line_at(y, shift):
    return pl.multiple_of(lax.rem(y - shift + SIDE, SIDE) * LINE, 256)


def col_at(x, shift):
    return pl.multiple_of(lax.rem(x + shift, SIDE) * HEAD, HEAD)


def seats(clips):
    lane = lax.broadcasted_iota(jnp.int32, (1, HEAD), 1)
    clip, frame = lax.shift_right_logical(lane, 3), lax.bitwise_and(lane, 7)
    first = clips[0, 0]
    second = first + clips[0, 1]
    total = second + clips[0, 2]
    start = jnp.where(clip == 0, 0, jnp.where(clip == 1, first, second))
    end = jnp.where(clip == 0, first, jnp.where(clip == 1, second, total))
    end = jnp.where(clip < 3, end, -1)
    start = start + frame * FRAME
    return start, jnp.minimum(end, start + FRAME), end


def key_features(clips, base, rows):
    start, end, _ = seats(clips)
    position = base + lax.broadcasted_iota(jnp.int32, (rows, HEAD), 0)
    return jnp.where((position >= start) & (position < end), 1.0, 0.0).astype(BF)


def query_features(clips, base, rows):
    start, _, end = seats(clips)
    position = base + lax.broadcasted_iota(jnp.int32, (rows, HEAD), 0)
    return jnp.where((position >= start) & (position < end), 0.0, FAR).astype(BF)


def to_row(column):
    n = column.shape[0]
    return jnp.transpose(jnp.broadcast_to(column, (n, 128)))[0:1]


def to_column(row):
    n = row.shape[1]
    return jnp.transpose(jnp.broadcast_to(row, (128, n)))[:, 0:1]


def place(x, pieces, target, base=0):
    for d in range(SIDE):
        target[pl.ds(pl.multiple_of(base + row_at(x, d), 64), ROWS), :HEAD] = pieces[d]


def gather_lines(x, y, lines, target, slot=None):
    for s in range(SIDE):
        base = line_at(y, s)
        for d in range(SIDE):
            piece = lines[s][d] if slot is None else lines[s][slot, d]
            target[pl.ds(pl.multiple_of(base + row_at(x, d), 64), ROWS), :HEAD] = piece


def forward_kernel(clips, q, kv0, kv1, kv2, kv3, out, lse, ks, vs, qs, os, scores):
    y, x = place_of()
    lines = (kv0, kv1, kv2, kv3)
    gather_lines(x, y, lines, ks, 0)
    gather_lines(x, y, lines, vs, 1)
    place(x, q, qs)
    qs[:, HEAD:] = query_features(clips, y * LINE, LINE)
    ks[:, HEAD:] = key_features(clips, 0, GROUP)
    for i in range(LINE // BLOCK):
        rows = pl.ds(i * BLOCK, BLOCK)
        q_block = qs[rows, :]
        top = jnp.full((BLOCK, 1), -jnp.inf, F32)
        for c in range(GROUP // CHUNK):
            at = pl.ds(c * CHUNK, CHUNK)
            s = nt(q_block, ks[at, :])
            scores[:, at] = s
            top = jnp.maximum(top, jnp.max(s, axis=1, keepdims=True))
        total = jnp.zeros((BLOCK, 1), F32)
        acc = jnp.zeros((BLOCK, HEAD), F32)
        for c in range(GROUP // CHUNK):
            at = pl.ds(c * CHUNK, CHUNK)
            p = jnp.exp2((scores[:, at] - top) * EXP_SCALE)
            total = total + jnp.sum(p, axis=1, keepdims=True)
            acc = acc + nn(p.astype(BF), vs[at, :])
        os[rows, :] = (acc / total).astype(BF)
        lse[0:1, rows] = to_row(top + jnp.log2(total) * (1.0 / EXP_SCALE))
    for d in range(SIDE):
        out[d] = os[pl.ds(row_at(x, d), ROWS), :]


def gradient_kernel(*refs):
    blocks, w, attention, outs, (keep, send, whole, cot) = (
        refs[:8],
        refs[8],
        refs[9],
        refs[10:14],
        refs[14:],
    )
    x = place_of()[1]
    z = lax.axis_index("tp")
    g = lax.axis_index("dp")

    def at(shift):
        return pl.ds(pl.multiple_of(lax.rem(z + shift + RING, RING) * WIDTH, WIDTH), WIDTH)

    cot[:, at(0)] = blocks[0][...]
    for s in range(1, 4):
        cot[:, at(-s)] = blocks[2 * s - 1][...]
        cot[:, at(s)] = blocks[2 * s][...]
    cot[:, at(-4)] = blocks[7][...]
    whole[...] = nt(cot[...], w[...]).astype(BF)
    for d, out in enumerate(outs):
        out[0] = whole[:, pl.ds(col_at(x, d), HEAD)]
        out[1] = attention[(SIDE - d) % SIDE]
    for c in range(SIDE * SIDE):
        low, high = cot[:, c * 256 : c * 256 + 128], cot[:, c * 256 + 128 : c * 256 + 256]
        keep[:, c * 128 : (c + 1) * 128] = jnp.where(g == 0, low, high)
        send[:, c * 128 : (c + 1) * 128] = jnp.where(g == 0, high, low)


def split3(row):
    high = row.astype(BF).astype(F32)
    middle = (row - high).astype(BF).astype(F32)
    return high, middle, row - high - middle


def delta_kernel(attention, lse, q, g0, g1, g2, g3, grads, stats, os, gs):
    x = place_of()[1]
    place(x, attention, os)
    for d, g in enumerate((g0, g1, g2, g3)):
        piece = g[0]
        gs[pl.ds(row_at(x, d), ROWS), :] = piece
        grads[d * ROWS : (d + 1) * ROWS, :] = piece
        grads[LINE + d * ROWS : LINE + (d + 1) * ROWS, :] = q[d]
    stats[...] = jnp.zeros(stats.shape, F32)
    stats[0:1, :] = lse[...]
    for i in range(LINE // BLOCK):
        rows = pl.ds(i * BLOCK, BLOCK)
        product = os[rows, :].astype(F32) * gs[rows, :].astype(F32)
        stats[1:2, rows] = to_row(jnp.sum(product, axis=1, keepdims=True))
    parts = split3(stats[0:1, :]) + split3(stats[1:2, :])
    tiles = [p[:, t * 128 : (t + 1) * 128] for p in parts for t in range(LINE // 128)]
    tiles.append(jnp.zeros((STAT_ROWS - len(tiles), 128), F32))
    grads[2 * LINE :, :] = jnp.concatenate(tiles, axis=0).astype(BF)


def read_stats(line):
    packed = line[2 * LINE :, :].astype(F32)
    n = LINE // 128
    rows = [
        jnp.concatenate([packed[r * n + t : r * n + t + 1] for t in range(n)], axis=1)
        for r in range(6)
    ]
    return rows[0] + (rows[1] + rows[2]), rows[3] + (rows[4] + rows[5])


def query_kernel(clips, q, grads, stats, kv0, kv1, kv2, kv3, out, ks, vs, qs, gs, ds):
    y, x = place_of()
    lines = (kv0, kv1, kv2, kv3)
    gather_lines(x, y, lines, ks, 0)
    gather_lines(x, y, lines, vs, 1)
    place(x, q, qs)
    place(x, tuple(grads[d * ROWS : (d + 1) * ROWS, :] for d in range(SIDE)), gs)
    qs[:, HEAD:] = query_features(clips, y * LINE, LINE)
    ks[:, HEAD:] = key_features(clips, 0, GROUP)
    for i in range(LINE // WIDE):
        rows = pl.ds(i * WIDE, WIDE)
        q_block, g_block = qs[rows, :], gs[rows, :]
        lse = to_column(stats[0:1, rows])
        delta = to_column(stats[1:2, rows])
        acc = jnp.zeros((WIDE, HEAD), F32)
        for c in range(GROUP // SLIM):
            at = pl.ds(c * SLIM, SLIM)
            p = jnp.exp2((nt(q_block, ks[at, :]) - lse) * EXP_SCALE)
            dp = nt(g_block, vs[at, :])
            acc = acc + nn((p * (dp - delta)).astype(BF), ks[at, :HEAD])
        ds[rows, :] = (acc * ROOT).astype(BF)
    for d in range(SIDE):
        out[d] = ds[pl.ds(row_at(x, d), ROWS), :]


def key_kernel(clips, kv0, g0, g1, g2, g3, dq, o0, o1, o2, o3, *scratch):
    qs, gs, st, ks, vs, dks, dvs = scratch
    y, x = place_of()
    for s, line in enumerate((g0, g1, g2, g3)):
        base = line_at(y, s)
        place(x, tuple(line[d * ROWS : (d + 1) * ROWS, :] for d in range(SIDE)), gs, base)
        place(
            x,
            tuple(line[LINE + d * ROWS : LINE + (d + 1) * ROWS, :] for d in range(SIDE)),
            qs,
            base,
        )
        lse, delta = read_stats(line)
        st[0:1, pl.ds(base, LINE)] = lse
        st[1:2, pl.ds(base, LINE)] = delta
    place(x, tuple(kv0[0, d] for d in range(SIDE)), ks)
    place(x, tuple(kv0[1, d] for d in range(SIDE)), vs)
    qs[:, HEAD:] = query_features(clips, 0, GROUP)
    ks[:, HEAD:] = key_features(clips, y * LINE, LINE)
    for i in range(LINE // WIDE):
        rows = pl.ds(i * WIDE, WIDE)
        k_block, v_block = ks[rows, :], vs[rows, :]
        dk = jnp.zeros((WIDE, HEAD), F32)
        dv = jnp.zeros((WIDE, HEAD), F32)
        for c in range(GROUP // SLIM):
            at = pl.ds(c * SLIM, SLIM)
            g_chunk = gs[at, :]
            p = jnp.exp2((nt(k_block, qs[at, :]) - st[0:1, at]) * EXP_SCALE)
            dv = dv + nn(p.astype(BF), g_chunk)
            dp = nt(v_block, g_chunk)
            dk = dk + nn((p * (dp - st[1:2, at])).astype(BF), qs[at, :HEAD])
        dks[rows, :] = (dk * ROOT).astype(BF)
        dvs[rows, :] = dv.astype(BF)
    for d, out in enumerate((o0, o1, o2, o3)):
        at = pl.ds(row_at(x, d), ROWS)
        out[0] = dq[d]
        out[1] = dks[at, :]
        out[2] = dvs[at, :]


def layer_kernel(a0, a1, a2, a3, w, cot, out, mine, attention):
    x = place_of()[1]
    for d, piece in enumerate((a0, a1, a2, a3)):
        attention[:, pl.ds(col_at(x, SIDE - d), HEAD)] = piece[1]
    whole = attention[...]
    mine[:, : FULL // 2] = cot[...]
    mine[:, FULL // 2 :] = whole
    for j in range(RING):
        at = pl.ds(j * WIDTH, WIDTH)
        out[:, at] = nn(whole, w[:, at]).astype(BF)


def weight_kernel(mine, other, cot, out):
    y, x = place_of()
    both = jnp.concatenate([mine[:, FULL // 2 :], other[:, FULL // 2 :]], axis=0)
    turned = jnp.transpose(both.astype(F32)).astype(BF)
    for row in range(SIDE):
        at = pl.ds(row * WIDTH, WIDTH)
        term = nn(turned[:, :ROWS], cot[:, at]) + nn(turned[:, ROWS:], other[:, at])
        dy = lax.rem(row - y + SIDE, SIDE)
        for column in range(SIDE):
            dx = lax.rem(column - x + SIDE, SIDE)
            out[dx, dy] = term[:, column * HEAD : (column + 1) * HEAD].astype(BF)


def unpack_kernel(*refs):
    x = place_of()[1]
    parts, (dq, dk, dv) = refs[0:4], refs[4:7]
    for d in range(SIDE):
        at = pl.ds(col_at(x, d), HEAD)
        dq[:, at] = parts[d][0]
        dk[:, at] = parts[d][1]
        dv[:, at] = parts[d][2]


X_SHIFT = {
    d: [(y * SIDE + x, y * SIDE + (x + d) % SIDE) for y in range(SIDE) for x in range(SIDE)]
    for d in range(-3, 4)
}
Y_SHIFT = {
    d: [(y * SIDE + x, ((y + d) % SIDE) * SIDE + x) for y in range(SIDE) for x in range(SIDE)]
    for d in range(-3, 4)
}

Z_SHIFT = {d: [(z, (z + d) % RING) for z in range(RING)] for d in (-1, 1)}


def move_x(a, d):
    return lax.ppermute(a, "ctx", X_SHIFT[d])


def move_y(a, d):
    return lax.ppermute(a, "ctx", Y_SHIFT[d])


def move_z(a, d):
    return lax.ppermute(a, "tp", Z_SHIFT[d])


def sum_all(terms):
    return functools.reduce(lambda a, b: a + b, [t.astype(F32) for t in terms]).astype(BF)


def after(a, *others):
    return lax.optimization_barrier((a, *others))[0]


def on_device(queries, keys, values, cotangent, w_out, clip_lengths):
    core = lax.axis_index("dp")
    swap = [(0, 1), (1, 0)]

    cot = cotangent[0]
    ahead1, behind1 = move_z(cot, 1), move_z(cot, -1)
    x = place_of()[1]
    packed = [
        jnp.stack(
            [
                lax.dynamic_slice(a[0], (0, lax.rem(x + d, SIDE) * HEAD), (ROWS, HEAD))
                for a in (queries, keys, values)
            ]
        )
        for d in range(SIDE)
    ]
    ahead2, behind2 = move_z(ahead1, 1), move_z(behind1, -1)
    line = jnp.stack([packed[0]] + [move_x(packed[d], d) for d in range(1, SIDE)], axis=1)
    q_own, kv_own = line[0], line[1:]
    kv = [kv_own] + [move_y(kv_own, d) for d in range(1, SIDE)]
    ahead3, behind3 = move_z(ahead2, 1), move_z(behind2, -1)
    ahead4 = move_z(ahead3, 1)
    blocks = [cot, ahead1, behind1, ahead2, behind2, ahead3, behind3, ahead4]
    kv = after(kv, ahead4)

    attention, lse = call(
        forward_kernel,
        (q_own, *kv),
        [sds(SIDE, ROWS, HEAD), sds(1, LINE, dtype=F32)],
        clips=clip_lengths,
        scratch=[
            pltpu.VMEM((GROUP, 2 * HEAD), BF),
            pltpu.VMEM((GROUP, HEAD), BF),
            pltpu.VMEM((LINE, 2 * HEAD), BF),
            pltpu.VMEM((LINE, HEAD), BF),
            pltpu.VMEM((BLOCK, GROUP), F32),
        ],
        name="forward",
        micros=5,
        room=10,
    )

    *grad_parts, cot_keep, cot_send = call(
        gradient_kernel,
        (*blocks, w_out, attention),
        [sds(2, ROWS, HEAD)] * SIDE + [sds(ROWS, FULL // 2)] * 2,
        scratch=[pltpu.VMEM((ROWS, WIDTH), BF), pltpu.VMEM((ROWS, FULL), BF)],
        name="gradient",
        micros=2,
    )
    mixed = [grad_parts[0]] + [move_x(grad_parts[d], d) for d in range(1, SIDE)]
    grads, stats = call(
        delta_kernel,
        (attention, lse, q_own, *mixed),
        [sds(2 * LINE + STAT_ROWS, HEAD), sds(8, LINE, dtype=F32)],
        scratch=[pltpu.VMEM((LINE, HEAD), BF), pltpu.VMEM((LINE, HEAD), BF)],
        name="delta",
    )
    grad_lines = [grads] + [move_y(grads, d) for d in range(1, SIDE)]
    partial, mine = call(
        layer_kernel,
        (*mixed, after(w_out, grads), cot_send),
        [sds(ROWS, FULL), sds(ROWS, FULL // 2 + WIDTH)],
        scratch=[pltpu.VMEM((ROWS, WIDTH), BF)],
        name="layer",
        micros=2,
    )
    layer_part = lax.psum_scatter(partial, "tp", scatter_dimension=1, tiled=True)

    term = call(
        weight_kernel,
        (after(mine, grads), lax.ppermute(mine, "dp", swap), cot_keep),
        [sds(SIDE, SIDE, WIDTH, HEAD)],
        name="weight",
        micros=2,
    )[0]
    dq = call(
        query_kernel,
        (q_own, grads, after(stats, term), *kv),
        [sds(SIDE, ROWS, HEAD)],
        clips=clip_lengths,
        scratch=[
            pltpu.VMEM((GROUP, 2 * HEAD), BF),
            pltpu.VMEM((GROUP, HEAD), BF),
            pltpu.VMEM((LINE, 2 * HEAD), BF),
            pltpu.VMEM((LINE, HEAD), BF),
            pltpu.VMEM((LINE, HEAD), BF),
        ],
        name="query",
        micros=5,
        room=9,
    )[0]
    up, down = move_x(term[2, :2], 1), move_x(term[2, 2:], -1)
    kv_key = after(kv_own, up, down)
    up = jnp.concatenate([term[1, :2] + up, term[1, 2:]], axis=0)
    down = jnp.concatenate([term[3, :2], term[3, 2:] + down], axis=0)
    term_parts = [term[0], move_x(up, 1), move_x(down, -1)]
    parts = call(
        key_kernel,
        (kv_key, *grad_lines, dq),
        [sds(3, ROWS, HEAD)] * SIDE,
        clips=clip_lengths,
        scratch=[
            pltpu.VMEM((GROUP, 2 * HEAD), BF),
            pltpu.VMEM((GROUP, HEAD), BF),
            pltpu.VMEM((8, GROUP), F32),
            pltpu.VMEM((LINE, 2 * HEAD), BF),
            pltpu.VMEM((LINE, HEAD), BF),
            pltpu.VMEM((LINE, HEAD), BF),
            pltpu.VMEM((LINE, HEAD), BF),
        ],
        name="key",
        micros=24,
        room=9,
    )
    term_parts = after(term_parts, parts)
    weight_part = sum_all(term_parts)
    weight_part = sum_all(
        [weight_part[0]] + [move_y(weight_part[d], d) for d in range(1, SIDE)]
    )
    other = lax.ppermute(weight_part, "dp", swap)
    first = core == 0
    weight_grad = jnp.concatenate(
        [jnp.where(first, weight_part, other), jnp.where(first, other, weight_part)], axis=1
    ).astype(F32)

    back = [parts[0]] + [move_x(parts[d], -d) for d in range(1, SIDE)]
    dq, dk, dv = call(unpack_kernel, back, [sds(ROWS, WIDTH)] * 3, name="unpack")
    return (layer_part[None], dq[None], dk[None], dv[None], weight_grad)


def solution(mesh):
    in_specs = (
        P("dp", "ctx", "tp"),
        P("dp", "ctx", "tp"),
        P("dp", "ctx", "tp"),
        P("dp", "ctx", "tp"),
        P("tp", None),
        P("dp", None),
    )
    out_specs = (
        P("dp", "ctx", "tp"),
        P("dp", "ctx", "tp"),
        P("dp", "ctx", "tp"),
        P("dp", "ctx", "tp"),
        P("tp", "ctx"),
    )
    return jax.shard_map(
        on_device, mesh=mesh, in_specs=in_specs, out_specs=out_specs, check_vma=False
    )
```

```python
import functools
import math

import jax
import jax.numpy as jnp
from jax import lax
from jax.experimental import pallas as pl
from jax.experimental.pallas import tpu as pltpu
from jax.sharding import PartitionSpec as P

HEAD = 128
FRAME = 512
SIDE = 4
ROWS = 192
LINE = SIDE * ROWS
GROUP = SIDE * LINE
HEADS_HERE = 4
WIDTH = HEADS_HERE * HEAD
RING = 8
FULL = RING * WIDTH
BLOCK = 256
CHUNK = 512
WIDE = 768
SLIM = 256
FAR = -1e9
ROOT = 1.0 / math.sqrt(HEAD)
STAT_ROWS = 48
EXP_SCALE = ROOT * math.log2(math.e)
BF = jnp.bfloat16
F32 = jnp.float32

VMEM = pl.BlockSpec(memory_space=pltpu.VMEM)
SMEM = pl.BlockSpec(memory_space=pltpu.SMEM)


def sds(*shape, dtype=BF):
    return jax.ShapeDtypeStruct(shape, dtype)


def call(kernel, args, outs, clips=None, scratch=(), micros=1, name=None, room=5, out_specs=None):
    lead = [] if clips is None else [clips]
    return pl.pallas_call(
        kernel,
        out_shape=outs,
        in_specs=[SMEM] * len(lead) + [VMEM] * len(args),
        out_specs=out_specs or [VMEM] * len(outs),
        scratch_shapes=list(scratch),
        compiler_params=pltpu.CompilerParams(vmem_limit_bytes=room * 2**20),
        cost_estimate=pl.CostEstimate(
            flops=int(micros * 1.15e9), bytes_accessed=2**20, transcendentals=0
        ),
        name=name,
    )(*lead, *args)


def place_of():
    ctx = lax.axis_index("ctx")
    return lax.div(ctx, SIDE), lax.rem(ctx, SIDE)


def nt(a, b):
    return lax.dot_general(a, b, (((1,), (1,)), ((), ())), preferred_element_type=F32)


def nn(a, b):
    return jnp.dot(a, b, preferred_element_type=F32)


def row_at(x, shift):
    return pl.multiple_of(lax.rem(x - shift + SIDE, SIDE) * ROWS, 64)


def line_at(y, shift):
    return pl.multiple_of(lax.rem(y - shift + SIDE, SIDE) * LINE, 256)


def col_at(x, shift):
    return pl.multiple_of(lax.rem(x + shift, SIDE) * HEAD, HEAD)


def seats(clips):
    lane = lax.broadcasted_iota(jnp.int32, (1, HEAD), 1)
    clip, frame = lax.shift_right_logical(lane, 3), lax.bitwise_and(lane, 7)
    first = clips[0, 0]
    second = first + clips[0, 1]
    total = second + clips[0, 2]
    start = jnp.where(clip == 0, 0, jnp.where(clip == 1, first, second))
    end = jnp.where(clip == 0, first, jnp.where(clip == 1, second, total))
    end = jnp.where(clip < 3, end, -1)
    start = start + frame * FRAME
    return start, jnp.minimum(end, start + FRAME), end


def key_features(clips, base, rows):
    start, end, _ = seats(clips)
    position = base + lax.broadcasted_iota(jnp.int32, (rows, HEAD), 0)
    return jnp.where((position >= start) & (position < end), 1.0, 0.0).astype(BF)


def query_features(clips, base, rows):
    start, _, end = seats(clips)
    position = base + lax.broadcasted_iota(jnp.int32, (rows, HEAD), 0)
    return jnp.where((position >= start) & (position < end), 0.0, FAR).astype(BF)


def to_row(column):
    n = column.shape[0]
    return jnp.transpose(jnp.broadcast_to(column, (n, 128)))[0:1]


def to_column(row):
    n = row.shape[1]
    return jnp.transpose(jnp.broadcast_to(row, (128, n)))[:, 0:1]


def place(x, pieces, target, base=0):
    for d in range(SIDE):
        target[pl.ds(pl.multiple_of(base + row_at(x, d), 64), ROWS), :HEAD] = pieces[d]


def gather_lines(x, y, lines, target, slot=None):
    for s in range(SIDE):
        base = line_at(y, s)
        for d in range(SIDE):
            piece = lines[s][d] if slot is None else lines[s][slot, d]
            target[pl.ds(pl.multiple_of(base + row_at(x, d), 64), ROWS), :HEAD] = piece


def forward_kernel(clips, q, kv0, kv1, kv2, kv3, out, lse, ks, vs, qs, os, scores):
    y, x = place_of()
    lines = (kv0, kv1, kv2, kv3)
    gather_lines(x, y, lines, ks, 0)
    gather_lines(x, y, lines, vs, 1)
    place(x, q, qs)
    qs[:, HEAD:] = query_features(clips, y * LINE, LINE)
    ks[:, HEAD:] = key_features(clips, 0, GROUP)
    for i in range(LINE // BLOCK):
        rows = pl.ds(i * BLOCK, BLOCK)
        q_block = qs[rows, :]
        top = jnp.full((BLOCK, 1), -jnp.inf, F32)
        for c in range(GROUP // CHUNK):
            at = pl.ds(c * CHUNK, CHUNK)
            s = nt(q_block, ks[at, :])
            scores[:, at] = s
            top = jnp.maximum(top, jnp.max(s, axis=1, keepdims=True))
        total = jnp.zeros((BLOCK, 1), F32)
        acc = jnp.zeros((BLOCK, HEAD), F32)
        for c in range(GROUP // CHUNK):
            at = pl.ds(c * CHUNK, CHUNK)
            p = jnp.exp2((scores[:, at] - top) * EXP_SCALE)
            total = total + jnp.sum(p, axis=1, keepdims=True)
            acc = acc + nn(p.astype(BF), vs[at, :])
        os[rows, :] = (acc / total).astype(BF)
        lse[0:1, rows] = to_row(top + jnp.log2(total) * (1.0 / EXP_SCALE))
    for d in range(SIDE):
        out[d] = os[pl.ds(row_at(x, d), ROWS), :]


def gradient_kernel(*refs):
    blocks, w, attention, outs, (keep, send, whole, cot) = (
        refs[:8],
        refs[8],
        refs[9],
        refs[10:14],
        refs[14:],
    )
    x = place_of()[1]
    z = lax.axis_index("tp")
    g = lax.axis_index("dp")

    def at(shift):
        return pl.ds(pl.multiple_of(lax.rem(z + shift + RING, RING) * WIDTH, WIDTH), WIDTH)

    cot[:, at(0)] = blocks[0][...]
    for s in range(1, 4):
        cot[:, at(-s)] = blocks[2 * s - 1][...]
        cot[:, at(s)] = blocks[2 * s][...]
    cot[:, at(-4)] = blocks[7][...]
    whole[...] = nt(cot[...], w[...]).astype(BF)
    for d, out in enumerate(outs):
        out[0] = whole[:, pl.ds(col_at(x, d), HEAD)]
        out[1] = attention[(SIDE - d) % SIDE]
    for c in range(SIDE * SIDE):
        low, high = cot[:, c * 256 : c * 256 + 128], cot[:, c * 256 + 128 : c * 256 + 256]
        keep[:, c * 128 : (c + 1) * 128] = jnp.where(g == 0, low, high)
        send[:, c * 128 : (c + 1) * 128] = jnp.where(g == 0, high, low)


def split3(row):
    high = row.astype(BF).astype(F32)
    middle = (row - high).astype(BF).astype(F32)
    return high, middle, row - high - middle


def delta_kernel(attention, lse, q, g0, g1, g2, g3, grads, stats, os, gs):
    x = place_of()[1]
    place(x, attention, os)
    for d, g in enumerate((g0, g1, g2, g3)):
        piece = g[0]
        gs[pl.ds(row_at(x, d), ROWS), :] = piece
        grads[d * ROWS : (d + 1) * ROWS, :] = piece
        grads[LINE + d * ROWS : LINE + (d + 1) * ROWS, :] = q[d]
    stats[...] = jnp.zeros(stats.shape, F32)
    stats[0:1, :] = lse[...]
    for i in range(LINE // BLOCK):
        rows = pl.ds(i * BLOCK, BLOCK)
        product = os[rows, :].astype(F32) * gs[rows, :].astype(F32)
        stats[1:2, rows] = to_row(jnp.sum(product, axis=1, keepdims=True))
    parts = split3(stats[0:1, :]) + split3(stats[1:2, :])
    tiles = [p[:, t * 128 : (t + 1) * 128] for p in parts for t in range(LINE // 128)]
    tiles.append(jnp.zeros((STAT_ROWS - len(tiles), 128), F32))
    grads[2 * LINE :, :] = jnp.concatenate(tiles, axis=0).astype(BF)


def read_stats(line):
    packed = line[2 * LINE :, :].astype(F32)
    n = LINE // 128
    rows = [
        jnp.concatenate([packed[r * n + t : r * n + t + 1] for t in range(n)], axis=1)
        for r in range(6)
    ]
    return rows[0] + (rows[1] + rows[2]), rows[3] + (rows[4] + rows[5])


def query_kernel(clips, q, grads, stats, kv0, kv1, kv2, kv3, out, ks, vs, qs, gs, ds):
    y, x = place_of()
    lines = (kv0, kv1, kv2, kv3)
    gather_lines(x, y, lines, ks, 0)
    gather_lines(x, y, lines, vs, 1)
    place(x, q, qs)
    place(x, tuple(grads[d * ROWS : (d + 1) * ROWS, :] for d in range(SIDE)), gs)
    qs[:, HEAD:] = query_features(clips, y * LINE, LINE)
    ks[:, HEAD:] = key_features(clips, 0, GROUP)
    for i in range(LINE // WIDE):
        rows = pl.ds(i * WIDE, WIDE)
        q_block, g_block = qs[rows, :], gs[rows, :]
        lse = to_column(stats[0:1, rows])
        delta = to_column(stats[1:2, rows])
        acc = jnp.zeros((WIDE, HEAD), F32)
        for c in range(GROUP // SLIM):
            at = pl.ds(c * SLIM, SLIM)
            p = jnp.exp2((nt(q_block, ks[at, :]) - lse) * EXP_SCALE)
            dp = nt(g_block, vs[at, :])
            acc = acc + nn((p * (dp - delta)).astype(BF), ks[at, :HEAD])
        ds[rows, :] = (acc * ROOT).astype(BF)
    for d in range(SIDE):
        out[d] = ds[pl.ds(row_at(x, d), ROWS), :]


def key_kernel(clips, kv0, g0, g1, g2, g3, dq, o0, o1, o2, o3, *scratch):
    qs, gs, st, ks, vs, dks, dvs = scratch
    y, x = place_of()
    for s, line in enumerate((g0, g1, g2, g3)):
        base = line_at(y, s)
        place(x, tuple(line[d * ROWS : (d + 1) * ROWS, :] for d in range(SIDE)), gs, base)
        place(
            x,
            tuple(line[LINE + d * ROWS : LINE + (d + 1) * ROWS, :] for d in range(SIDE)),
            qs,
            base,
        )
        lse, delta = read_stats(line)
        st[0:1, pl.ds(base, LINE)] = lse
        st[1:2, pl.ds(base, LINE)] = delta
    place(x, tuple(kv0[0, d] for d in range(SIDE)), ks)
    place(x, tuple(kv0[1, d] for d in range(SIDE)), vs)
    qs[:, HEAD:] = query_features(clips, 0, GROUP)
    ks[:, HEAD:] = key_features(clips, y * LINE, LINE)
    for i in range(LINE // WIDE):
        rows = pl.ds(i * WIDE, WIDE)
        k_block, v_block = ks[rows, :], vs[rows, :]
        dk = jnp.zeros((WIDE, HEAD), F32)
        dv = jnp.zeros((WIDE, HEAD), F32)
        for c in range(GROUP // SLIM):
            at = pl.ds(c * SLIM, SLIM)
            g_chunk = gs[at, :]
            p = jnp.exp2((nt(k_block, qs[at, :]) - st[0:1, at]) * EXP_SCALE)
            dv = dv + nn(p.astype(BF), g_chunk)
            dp = nt(v_block, g_chunk)
            dk = dk + nn((p * (dp - st[1:2, at])).astype(BF), qs[at, :HEAD])
        dks[rows, :] = (dk * ROOT).astype(BF)
        dvs[rows, :] = dv.astype(BF)
    for d, out in enumerate((o0, o1, o2, o3)):
        at = pl.ds(row_at(x, d), ROWS)
        out[0] = dq[d]
        out[1] = dks[at, :]
        out[2] = dvs[at, :]


def layer_kernel(a0, a1, a2, a3, w, cot, out, mine, attention, ready, sems):
    x = place_of()[1]
    for d, piece in enumerate((a0, a1, a2, a3)):
        attention[:, pl.ds(col_at(x, SIDE - d), HEAD)] = piece[1]
    whole = attention[...]
    mine[:, : FULL // 2] = cot[...]
    mine[:, FULL // 2 :] = whole
    copies = []
    for j in range(RING):
        at = pl.ds(j * WIDTH, WIDTH)
        ready[j] = nn(whole, w[:, at]).astype(BF)
        copies.append(pltpu.make_async_copy(ready.at[j], out.at[:, at], sems.at[j]))
        copies[j].start()
    for copy in copies:
        copy.wait()


def weight_kernel(mine, other, cot, out):
    y, x = place_of()
    both = jnp.concatenate([mine[:, FULL // 2 :], other[:, FULL // 2 :]], axis=0)
    turned = jnp.transpose(both.astype(F32)).astype(BF)
    for row in range(SIDE):
        at = pl.ds(row * WIDTH, WIDTH)
        term = nn(turned[:, :ROWS], cot[:, at]) + nn(turned[:, ROWS:], other[:, at])
        dy = lax.rem(row - y + SIDE, SIDE)
        for column in range(SIDE):
            dx = lax.rem(column - x + SIDE, SIDE)
            out[dx, dy] = term[:, column * HEAD : (column + 1) * HEAD].astype(BF)


def last_kernel(p0, p1, p2, p3, mine, other, dq, dk, dv, dw):
    x = place_of()[1]
    g = lax.axis_index("dp")
    for d, part in enumerate((p0, p1, p2, p3)):
        at = pl.ds(col_at(x, d), HEAD)
        dq[:, at] = part[0]
        dk[:, at] = part[1]
        dv[:, at] = part[2]
    own, far = mine[...].astype(F32), other[...].astype(F32)
    dw[:, :HEAD] = jnp.where(g == 0, own, far)
    dw[:, HEAD:] = jnp.where(g == 0, far, own)


X_SHIFT = {
    d: [(y * SIDE + x, y * SIDE + (x + d) % SIDE) for y in range(SIDE) for x in range(SIDE)]
    for d in range(-3, 4)
}
Y_SHIFT = {
    d: [(y * SIDE + x, ((y + d) % SIDE) * SIDE + x) for y in range(SIDE) for x in range(SIDE)]
    for d in range(-3, 4)
}

Z_SHIFT = {d: [(z, (z + d) % RING) for z in range(RING)] for d in (-1, 1)}


def move_x(a, d):
    return lax.ppermute(a, "ctx", X_SHIFT[d])


def move_y(a, d):
    return lax.ppermute(a, "ctx", Y_SHIFT[d])


def move_z(a, d):
    return lax.ppermute(a, "tp", Z_SHIFT[d])


def sum_all(terms):
    return functools.reduce(lambda a, b: a + b, [t.astype(F32) for t in terms]).astype(BF)


def after(a, *others):
    return lax.optimization_barrier((a, *others))[0]


def on_device(queries, keys, values, cotangent, w_out, clip_lengths):
    swap = [(0, 1), (1, 0)]

    cot = cotangent[0]
    ahead1, behind1 = move_z(cot, 1), move_z(cot, -1)
    x = place_of()[1]
    packed = [
        jnp.stack(
            [
                lax.dynamic_slice(a[0], (0, lax.rem(x + d, SIDE) * HEAD), (ROWS, HEAD))
                for a in (queries, keys, values)
            ]
        )
        for d in range(SIDE)
    ]
    ahead2, behind2 = move_z(ahead1, 1), move_z(behind1, -1)
    line = jnp.stack([packed[0]] + [move_x(packed[d], d) for d in range(1, SIDE)], axis=1)
    q_own, kv_own = line[0], line[1:]
    kv = [kv_own] + [move_y(kv_own, d) for d in range(1, SIDE)]
    ahead3, behind3 = move_z(ahead2, 1), move_z(behind2, -1)
    ahead4 = move_z(ahead3, 1)
    blocks = [cot, ahead1, behind1, ahead2, behind2, ahead3, behind3, ahead4]
    kv = after(kv, ahead4)

    attention, lse = call(
        forward_kernel,
        (q_own, *kv),
        [sds(SIDE, ROWS, HEAD), sds(1, LINE, dtype=F32)],
        clips=clip_lengths,
        scratch=[
            pltpu.VMEM((GROUP, 2 * HEAD), BF),
            pltpu.VMEM((GROUP, HEAD), BF),
            pltpu.VMEM((LINE, 2 * HEAD), BF),
            pltpu.VMEM((LINE, HEAD), BF),
            pltpu.VMEM((BLOCK, GROUP), F32),
        ],
        name="forward",
        micros=5,
        room=10,
    )

    *grad_parts, cot_keep, cot_send = call(
        gradient_kernel,
        (*blocks, w_out, attention),
        [sds(2, ROWS, HEAD)] * SIDE + [sds(ROWS, FULL // 2)] * 2,
        scratch=[pltpu.VMEM((ROWS, WIDTH), BF), pltpu.VMEM((ROWS, FULL), BF)],
        name="gradient",
        micros=2,
    )
    mixed = [grad_parts[0]] + [move_x(grad_parts[d], d) for d in range(1, SIDE)]
    grads, stats = call(
        delta_kernel,
        (attention, lse, q_own, *mixed),
        [sds(2 * LINE + STAT_ROWS, HEAD), sds(8, LINE, dtype=F32)],
        scratch=[pltpu.VMEM((LINE, HEAD), BF), pltpu.VMEM((LINE, HEAD), BF)],
        name="delta",
    )
    grad_lines = [grads] + [move_y(grads, d) for d in range(1, SIDE)]
    partial, mine = call(
        layer_kernel,
        (*mixed, after(w_out, grads), cot_send),
        [sds(ROWS, FULL), sds(ROWS, FULL // 2 + WIDTH)],
        scratch=[
            pltpu.VMEM((ROWS, WIDTH), BF),
            pltpu.VMEM((RING, ROWS, WIDTH), BF),
            pltpu.SemaphoreType.DMA((RING,)),
        ],
        out_specs=[pl.BlockSpec(memory_space=pl.ANY), VMEM],
        name="layer",
        micros=2,
    )
    layer_part = lax.psum_scatter(partial, "tp", scatter_dimension=1, tiled=True)

    term = call(
        weight_kernel,
        (after(mine, grads), lax.ppermute(mine, "dp", swap), cot_keep),
        [sds(SIDE, SIDE, WIDTH, HEAD)],
        name="weight",
        micros=2,
    )[0]
    dq = call(
        query_kernel,
        (q_own, grads, after(stats, term), *kv),
        [sds(SIDE, ROWS, HEAD)],
        clips=clip_lengths,
        scratch=[
            pltpu.VMEM((GROUP, 2 * HEAD), BF),
            pltpu.VMEM((GROUP, HEAD), BF),
            pltpu.VMEM((LINE, 2 * HEAD), BF),
            pltpu.VMEM((LINE, HEAD), BF),
            pltpu.VMEM((LINE, HEAD), BF),
        ],
        name="query",
        micros=5,
        room=9,
    )[0]
    up, down = move_x(term[2, :2], 1), move_x(term[2, 2:], -1)
    kv_key = after(kv_own, up, down)
    up = jnp.concatenate([term[1, :2] + up, term[1, 2:]], axis=0)
    down = jnp.concatenate([term[3, :2], term[3, 2:] + down], axis=0)
    term_parts = [term[0], move_x(up, 1), move_x(down, -1)]
    parts = call(
        key_kernel,
        (kv_key, *grad_lines, dq),
        [sds(3, ROWS, HEAD)] * SIDE,
        clips=clip_lengths,
        scratch=[
            pltpu.VMEM((GROUP, 2 * HEAD), BF),
            pltpu.VMEM((GROUP, HEAD), BF),
            pltpu.VMEM((8, GROUP), F32),
            pltpu.VMEM((LINE, 2 * HEAD), BF),
            pltpu.VMEM((LINE, HEAD), BF),
            pltpu.VMEM((LINE, HEAD), BF),
            pltpu.VMEM((LINE, HEAD), BF),
        ],
        name="key",
        micros=24,
        room=9,
    )
    term_parts = after(term_parts, parts)
    weight_part = sum_all(term_parts)
    weight_part = sum_all(
        [weight_part[0]] + [move_y(weight_part[d], d) for d in range(1, SIDE)]
    )
    other = lax.ppermute(weight_part, "dp", swap)

    back = [parts[0]] + [move_x(parts[d], -d) for d in range(1, SIDE)]
    dq, dk, dv, weight_grad = call(
        last_kernel,
        (*back, weight_part, other),
        [sds(ROWS, WIDTH)] * 3 + [sds(WIDTH, 2 * HEAD, dtype=F32)],
        name="last",
    )
    return (layer_part[None], dq[None], dk[None], dv[None], weight_grad)


def solution(mesh):
    in_specs = (
        P("dp", "ctx", "tp"),
        P("dp", "ctx", "tp"),
        P("dp", "ctx", "tp"),
        P("dp", "ctx", "tp"),
        P("tp", None),
        P("dp", None),
    )
    out_specs = (
        P("dp", "ctx", "tp"),
        P("dp", "ctx", "tp"),
        P("dp", "ctx", "tp"),
        P("dp", "ctx", "tp"),
        P("tp", "ctx"),
    )
    return jax.shard_map(
        on_device, mesh=mesh, in_specs=in_specs, out_specs=out_specs, check_vma=False
    )
```
